128 devices in a mesh: tm: 16 (over x_lo, y, core), chan: 8 (over z, x_hi).
Axes of the slice: x: 4 (x_hi: 2, x_lo: 2; x = x_hi * 2 + x_lo), y: 4, z: 4, core: 2. Of those that a mesh axis runs over, the one named last changes fastest.
Arguments:
- frames: bfloat16 [32768, 1280], P('tm', 'chan'), may hold values from -64 to 64
- up_weight: bfloat16 [1280, 5120], P('tm', 'chan'), may hold values from -0.15625 to 0.15625
- down_weight: bfloat16 [5120, 1280], P('chan', 'tm'), may hold values from -0.078125 to 0.078125
- ffn_gain: float32 [1280], replicated, may hold values from 0.1 to 1.9
- final_gain: float32 [1280], replicated, may hold values from 0.5 to 1.5
- ctc_weight: bfloat16 [1280, 256], replicated, may hold values from -12 to 12
- labels: int32 [8192], replicated, may hold values from 0 to 255, as said below
- starts: int32 [128], replicated, may hold values from 0 to 7936, as said below
- widths: int32 [128], replicated, may hold values from 64 to 128
Outputs:
- emissions: float32 [32768, 256], P(('tm', 'chan'))
- band_scores: float32 [128, 128], P(('tm', 'chan'))
The draws below stay inside these ranges and needn't reach their ends.
Inputs may be any that keep to these rules, and one draw needn't show every extreme that they name: `labels`: every even state has id 0. Never falling; starts[0] and each rise from one entry to the next are at most 128; the last entry is the largest.
All inputs are finite; a program needn't handle non-finite values.
Results may differ from the reference program's by a relative error of at most 0.0023.
Values may be sent and summed in bfloat16 or wider, within the bound.
A program may use at most 64 MiB of HBM per device.

```python
import jax
import jax.numpy as jnp
from jax import lax

D = 1280
FF = 5120
V = 256
S = 8192
BAND = 128
FD = 256
SHARDS = 128
FRAMES = 32768


BLANK_LEAN = 26.0


def common_direction(key):
    return jax.random.normal(jax.random.fold_in(key, 9), (1, D), jnp.float32)


def draw_frames(key, part):
    keys = jax.random.split(jax.random.fold_in(key, 1), 1)
    common = common_direction(key)
    values = jnp.clip(jax.random.normal(keys[0], (FRAMES, D), jnp.float32), -6.0, 6.0) + common
    values = jnp.clip(values, -64.0, 64.0)
    return values.astype(jnp.bfloat16)


def draw_ctc_weight(key, part):
    keys = jax.random.split(jax.random.fold_in(key, 2), 1)
    spread = 3.0 / D ** 0.5
    lean_col = BLANK_LEAN * common_direction(key)[0] / D
    values = jnp.clip(jax.random.normal(keys[0], (D, V), jnp.float32), -6.0, 6.0) * spread
    values = values.at[:, 0].set(lean_col + 0.5 * values[:, 0])
    return values.astype(jnp.bfloat16)


def draw_labels(key, part):
    states = jnp.arange(S, dtype=jnp.int32)
    chars = jax.random.randint(jax.random.fold_in(key, 3), (S,), 1, V, dtype=jnp.int32)
    return jnp.where(states % 2 == 0, 0, chars).astype(jnp.int32)


def draw_starts(key, part):
    top = min(S - 2 * BAND, (SHARDS - 1) * (BAND // 2))
    need = -(-top // BAND)
    flat_most = SHARDS - need
    flat_len = flat_most // 2 + jax.random.randint(jax.random.fold_in(key, 4), (), 0, flat_most // 4 + 1, dtype=jnp.int32)
    flat_len = jnp.maximum(flat_len, 1).astype(jnp.int32)
    first = jax.random.randint(jax.random.fold_in(key, 5), (), 0, BAND // 2 + 1, dtype=jnp.int32)
    first = jnp.minimum(first, top).astype(jnp.int32)
    rising = (SHARDS - flat_len).astype(jnp.int32)
    step_most = (top - first + rising - 1) // rising
    shard_ids = jnp.arange(SHARDS, dtype=jnp.int32)
    since = jnp.maximum(shard_ids - (flat_len - 1), 0)
    base = first + since * (top - first) // rising
    jitter = jax.random.randint(jax.random.fold_in(key, 10), (SHARDS,), 0, BAND - step_most + 1, dtype=jnp.int32)
    jitter = jnp.where((shard_ids < flat_len) | (shard_ids == SHARDS - 1), 0, jitter)
    raised = jnp.minimum(base + jitter, top)
    return jax.lax.cummax(raised, axis=0).astype(jnp.int32)


def draw_widths(key, part):
    values = jax.random.randint(jax.random.fold_in(key, 6), (SHARDS,), BAND // 2, BAND + 1, dtype=jnp.int32)
    forced = jax.random.randint(jax.random.fold_in(key, 8), (), 0, SHARDS, dtype=jnp.int32)
    return jnp.where(jnp.arange(SHARDS, dtype=jnp.int32) == forced, BAND, values).astype(jnp.int32)


def steps_of(rng, shape, shards, smallest, largest):
    loudness = 1.0
    for axis_at, parts in shards:
        heights = jax.random.uniform(jax.random.fold_in(jax.random.fold_in(rng, 6), axis_at), (parts,), jnp.float32, smallest / len(shards), largest / len(shards))
        loudness = loudness * jnp.repeat(jnp.exp(heights), shape[axis_at] // parts).reshape((-1,) + (1,) * (len(shape) - 1 - axis_at))
    return loudness


def scatter_about(rng, dims, deviation, reach, cuts=(), held_as=jnp.bfloat16):
    values = deviation * jax.random.normal(rng, dims, jnp.float32)
    if cuts:
        values = values * steps_of(rng, dims, cuts, -0.22, 0.18)
    return jnp.clip(values, -reach, reach).astype(held_as)


def setup_inputs(seed: int = 0) -> dict:
    splits = jax.random.split(jax.random.key(seed), 10)
    return {
        "frames": draw_frames(jax.random.fold_in(splits[9], 71), 0),
        "up_weight": scatter_about(splits[1], (D, FF), D ** -0.5, 0.15625, ((0, 16), (1, 8))),
        "down_weight": scatter_about(splits[2], (FF, D), FF ** -0.5, 0.078125, ((0, 8), (1, 16))),
        "ffn_gain": jnp.clip(1.0 + 0.18 * jax.random.normal(splits[3], (D,), jnp.float32), 0.1, 1.9),
        "final_gain": jnp.clip(1.0 + 0.1 * jax.random.normal(splits[4], (D,), jnp.float32), 0.5, 1.5),
        "ctc_weight": draw_ctc_weight(jax.random.fold_in(splits[9], 71), 0),
        "labels": draw_labels(jax.random.fold_in(splits[9], 71), 0),
        "starts": draw_starts(jax.random.fold_in(splits[9], 71), 0),
        "widths": draw_widths(jax.random.fold_in(splits[9], 71), 0),
    }


LN_EPSILON = 1e-05
NEG_SCORE = -1000000000.0

def layer_norm(values, gain_row):
    row_mean = lax.optimization_barrier(jnp.mean(values, axis=-1, keepdims=True))
    row_var = lax.optimization_barrier(jnp.mean(jnp.square(values - row_mean), axis=-1, keepdims=True))
    return (values - row_mean) * lax.rsqrt(row_var + LN_EPSILON) * gain_row

def reference(frames, up_weight, down_weight, ffn_gain, final_gain, ctc_weight, labels, starts, widths):

    def shard_emissions(shard_rows):
        normed_in = layer_norm(shard_rows.astype(jnp.float32), ffn_gain).astype(jnp.bfloat16)
        pre_act = jnp.dot(normed_in, up_weight, preferred_element_type=jnp.float32)
        hidden = jax.nn.silu(pre_act).astype(jnp.bfloat16)
        branch = jnp.dot(hidden, down_weight, preferred_element_type=jnp.float32)
        residual = shard_rows.astype(jnp.float32) + 0.5 * branch
        normed = layer_norm(residual, final_gain).astype(jnp.bfloat16)
        logits = jnp.dot(normed, ctc_weight, preferred_element_type=jnp.float32)
        return jax.nn.log_softmax(logits, axis=-1)
    per_shard = lax.map(shard_emissions, frames.reshape(SHARDS, FD, D))
    emissions = per_shard.reshape(FRAMES, V)
    band_index = jnp.arange(BAND, dtype=jnp.int32)
    window = jnp.arange(2 * BAND, dtype=jnp.int32)
    scale_out = 1.0 / FRAMES

    def shard_step(vector, shard_item):
        shard_index, shard_emit = shard_item
        prior_shard = jnp.maximum(shard_index - 1, 0)
        start_in = jnp.where(shard_index > 0, starts[prior_shard], 0).astype(jnp.int32)
        width_in = jnp.where(shard_index > 0, widths[prior_shard], 2).astype(jnp.int32)
        window_ids = lax.dynamic_slice_in_dim(labels, start_in, 2 * BAND)
        before = jnp.concatenate([jnp.full((2,), -1, jnp.int32), window_ids[:-2]])
        skip_ok = (window >= 2) & (window_ids != before)
        scores = jnp.take(shard_emit, window_ids, axis=1)
        entry_scores = jnp.where(band_index < width_in, vector, NEG_SCORE)
        path_state = jnp.concatenate([entry_scores, jnp.full((BAND,), NEG_SCORE, jnp.float32)])

        def frame_step(path_state, frame_emit):
            from_one = jnp.concatenate([jnp.full((1,), NEG_SCORE, jnp.float32), path_state[:-1]])
            from_two = jnp.concatenate([jnp.full((2,), NEG_SCORE, jnp.float32), path_state[:-2]])
            from_two = jnp.where(skip_ok, from_two, NEG_SCORE)
            return (jnp.maximum(jnp.maximum(path_state, from_one), from_two) + frame_emit, None)
        path_state, _ = lax.scan(frame_step, path_state, scores)
        offset = (starts[shard_index] - start_in).astype(jnp.int32)
        exit_scores = lax.dynamic_slice_in_dim(path_state, offset, BAND)
        live_cols = band_index < widths[shard_index]
        vector = jnp.where(live_cols, exit_scores, NEG_SCORE)
        band_row = jnp.where(live_cols, exit_scores * scale_out, 0.0)
        return (vector, band_row)
    initial = jnp.where(band_index < 2, 0.0, NEG_SCORE).astype(jnp.float32)
    _, band_scores = lax.scan(shard_step, initial, (jnp.arange(SHARDS, dtype=jnp.int32), per_shard))
    return (emissions, band_scores)
```

```python
import functools

import jax
import jax.numpy as jnp
from jax import lax
from jax.experimental import pallas as pl
from jax.experimental.pallas import tpu as pltpu
from jax.sharding import PartitionSpec as P

BAND = 128
LN_EPSILON = 1e-05
NEG = -1e30
MESH = pl.DeviceIdType.MESH
ANY = pl.BlockSpec(memory_space=pl.ANY)
VM = pl.BlockSpec(memory_space=pltpu.VMEM)
MIB = 2**20


def position():
    tm, chan = lax.axis_index("tm"), lax.axis_index("chan")
    x = lax.rem(chan, 2) * 2 + tm // 8
    return x, lax.rem(tm // 2, 4), chan // 2, lax.rem(tm, 2)


def device(x, y, z, core):
    return (lax.rem(x, 2) * 8 + y * 2 + core, z * 2 + x // 2)


def moved(pos, axis, by):
    out = list(pos)
    out[axis] = lax.rem(pos[axis] + by + 4, 4)
    return tuple(out)


PARTS = ((0, 64, (2, 0, 1)), (64, 48, (1, 2, 0)), (112, 48, (0, 1, 2)))
STEPS = (0, -1, 1, 2)


def block_at(w, pos, part):
    x, y, z, core = pos
    row, rows, _ = part
    return w.at[z, x // 2, lax.rem(x, 2), y, core, pl.ds(row, rows)]


def column_at(w, pos, part):
    x, y, z, core = pos
    row, rows, (axis, _, _) = part
    if axis == 0:
        return w.at[z, :, :, y, core, pl.ds(row, rows)]
    if axis == 1:
        return w.at[z, x // 2, lax.rem(x, 2), :, core, pl.ds(row, rows)]
    return w.at[:, x // 2, lax.rem(x, 2), y, core, pl.ds(row, rows)]


def gather_kernel(frames, chunk, w, mine, local_sem, fr_send, fr_recv, s1, r1, s2, r2, s3, r3, sc, rc):
    me = position()
    x, y, z, core = me
    tm, chan = lax.axis_index("tm"), lax.axis_index("chan")
    sibling = (tm + 1 - 2 * core, chan)

    barrier = pltpu.get_barrier_semaphore()
    for axis in range(3):
        for by in (1, -1):
            pl.semaphore_signal(barrier, inc=1, device_id=device(*moved(me, axis, by)), device_id_type=MESH)
    pl.semaphore_signal(barrier, inc=1, device_id=sibling, device_id_type=MESH)
    for d in range(1, 8):
        pl.semaphore_signal(barrier, inc=1, device_id=(tm, lax.rem(chan + d, 8)), device_id_type=MESH)
    pl.semaphore_wait(barrier, 14)

    pending = []

    def send(src, dst, send_sem, recv_sem, to):
        copy = pltpu.make_async_remote_copy(
            src_ref=src, dst_ref=dst, send_sem=send_sem, recv_sem=recv_sem, device_id=to, device_id_type=MESH
        )
        copy.start()
        pending.append(copy)

    def arrived(ref, sem):
        pltpu.make_async_copy(ref, ref, sem).wait()

    own = pltpu.make_async_copy(chunk, w.at[z, x // 2, lax.rem(x, 2), y, core], local_sem.at[0])
    own.start()
    for d in range(1, 8):
        peer = lax.rem(chan + d, 8)
        send(
            frames.at[pl.ds(peer * 256, 256)], mine.at[chan], fr_send.at[d - 1], fr_recv.at[d - 1], (tm, peer)
        )
    own_frames = pltpu.make_async_copy(frames.at[pl.ds(chan * 256, 256)], mine.at[chan], local_sem.at[1])
    own_frames.start()
    own.wait()

    def to_sibling(p, k, ref):
        send(ref, ref, sc.at[p, k], rc.at[p, k], sibling)

    def phase_sends(ref, axis, send_sems, recv_sems):
        send(ref, ref, send_sems(0), recv_sems(1), device(*moved(me, axis, 1)))
        send(ref, ref, send_sems(1), recv_sems(2), device(*moved(me, axis, -1)))

    for p, part in enumerate(PARTS):
        block = block_at(w, me, part)
        phase_sends(block, part[2][0], lambda k: s1.at[p, k], lambda k: r1.at[p, k])
        phase_sends(block, part[2][1], lambda k: s2.at[p, 0, k], lambda k: r2.at[p, 0, k])
    for k in (1, 2, 3):
        for p, part in enumerate(PARTS):
            a, b, _ = part[2]
            at = moved(me, a, STEPS[k])
            block = block_at(w, at, part)
            arrived(block, r1.at[p, k])
            if k == 1 + p % 2:
                send(block, block, s1.at[p, 2], r1.at[p, 3], device(*moved(me, a, -STEPS[k])))
            phase_sends(block, b, lambda q: s2.at[p, k, q], lambda q: r2.at[p, k, q])
    for p, part in enumerate(PARTS):
        column = column_at(w, me, part)
        phase_sends(column, part[2][2], lambda q: s3.at[p, 0, q], lambda q: r3.at[p, 0, q])
        to_sibling(p, 0, column)
    for j in (1, 2, 3):
        for p, part in enumerate(PARTS):
            a, b, c = part[2]
            for k in range(4):
                at = moved(moved(me, b, STEPS[j]), a, STEPS[k])
                block = block_at(w, at, part)
                arrived(block, r2.at[p, k, j])
                if j == 1 + k % 2:
                    send(block, block, s2.at[p, k, 2], r2.at[p, k, 3], device(*moved(me, b, -STEPS[j])))
            column = column_at(w, moved(me, b, STEPS[j]), part)
            phase_sends(column, c, lambda q: s3.at[p, j, q], lambda q: r3.at[p, j, q])
            to_sibling(p, j, column)
    for i in (1, 2, 3):
        for j in range(4):
            for p, part in enumerate(PARTS):
                _, b, c = part[2]
                column = column_at(w, moved(moved(me, c, STEPS[i]), b, STEPS[j]), part)
                arrived(column, r3.at[p, j, i])
                if i == 1 + j % 2:
                    send(column, column, s3.at[p, j, 2], r3.at[p, j, 3], device(*moved(me, c, -STEPS[i])))
                to_sibling(p, 4 * i + j, column)
    other = (x, y, z, 1 - core)
    for i in range(4):
        for j in range(4):
            for p, part in enumerate(PARTS):
                _, b, c = part[2]
                column = column_at(w, moved(moved(other, c, STEPS[i]), b, STEPS[j]), part)
                arrived(column, rc.at[p, 4 * i + j])
    own_frames.wait()
    for d in range(1, 8):
        src = lax.rem(chan + 8 - d, 8)
        arrived(mine.at[src], fr_recv.at[d - 1])
    for copy in pending:
        copy.wait_send()


def gather(frames, chunk):
    dma = pltpu.SemaphoreType.DMA
    return pl.pallas_call(
        gather_kernel,
        out_shape=(
            jax.ShapeDtypeStruct((4, 2, 2, 4, 2, 160, 640), jnp.bfloat16),
            jax.ShapeDtypeStruct((8, 256, 160), jnp.bfloat16),
        ),
        in_specs=[ANY, ANY],
        out_specs=(ANY, ANY),
        scratch_shapes=[
            dma((2,)), dma((7,)), dma((7,)),
            dma((3, 3)), dma((3, 4)),
            dma((3, 4, 3)), dma((3, 4, 4)),
            dma((3, 4, 3)), dma((3, 4, 4)),
            dma((3, 16)), dma((3, 16)),
        ],
        compiler_params=pltpu.CompilerParams(collective_id=1, has_side_effects=True),
        name="gather",
    )(frames, chunk)


def norm_rows(values, gain_row):
    row_mean = jnp.mean(values, axis=-1, keepdims=True)
    centred = values - row_mean
    row_var = jnp.mean(jnp.square(centred), axis=-1, keepdims=True)
    return centred * lax.rsqrt(row_var + LN_EPSILON) * gain_row


def split(values):
    high = values.astype(jnp.bfloat16)
    return high, (values - high.astype(jnp.float32)).astype(jnp.bfloat16)


NT = (((1,), (1,)), ((), ()))


def viterbi(scal, emissions, ids, states):
    par, width_in, offset, width_out = scal[0], scal[1], scal[2], scal[3]
    char = lax.broadcasted_iota(jnp.int32, (128, 256), 1)
    choose = (ids[:, 0:1] == char).astype(jnp.float32) - (char == 0).astype(jnp.float32)
    choose = choose.astype(jnp.bfloat16)
    parts = list(split(emissions))
    parts.append((emissions - parts[0].astype(jnp.float32) - parts[1].astype(jnp.float32)).astype(jnp.bfloat16))
    gain = sum(lax.dot_general(choose, part, NT, preferred_element_type=jnp.float32) for part in parts)
    blank = jnp.sum(emissions[:, 0:1])
    skip = jnp.broadcast_to(jnp.where(ids[:, 0:1] == ids[:, 1:2], NEG, 0.0), (128, 128)).reshape(16, 8, 128)
    v = lax.broadcasted_iota(jnp.int32, (16, 8, 128), 0)
    sub = lax.broadcasted_iota(jnp.int32, (16, 8, 128), 1)
    start = lax.broadcasted_iota(jnp.int32, (16, 8, 128), 2)
    at = 2 * (sub * 16 + v) - par
    live = start < width_in
    even = jnp.where((at == start) & live, 0.0, NEG)
    odd = jnp.where((at + 1 == start) & live, 0.0, NEG)
    top = jnp.full((8, 128), NEG, jnp.float32)
    first = lax.broadcasted_iota(jnp.int32, (8, 128), 0) == 0
    for half in range(2):
        block = gain[:, half * 128 : half * 128 + 128].reshape(16, 8, 128)
        for t in range(128):
            step = jnp.broadcast_to(block[:, :, t : t + 1], (16, 8, 128))
            turned = pltpu.roll(odd[15], 1, 0)
            below = jnp.concatenate([jnp.where(first, NEG, turned)[None], odd[:15]], axis=0)
            top = jnp.maximum(top, turned)
            odd = jnp.maximum(jnp.maximum(odd, even), below + skip) + step
            even = jnp.maximum(even, below)
    for k in range(16):
        states[pl.ds(2 * k, 8, stride=32), :] = even[k]
        states[pl.ds(2 * k + 1, 8, stride=32), :] = odd[k]
    states[256:264, :] = top
    reached = states[pl.ds(par + offset, 128), :]
    row = lax.broadcasted_iota(jnp.int32, (128, 128), 0)
    reached = jnp.where(row < width_out, reached + blank, NEG)
    return jnp.transpose(reached)


def local_kernel(scal, w, mine, ffn_gain, final_gain, ctc, ids, emis, transfer, x_in, normed_in, total, states):
    step = pl.program_id(0)

    @pl.when(step == 0)
    def _():
        x_in[...] = jnp.concatenate([mine[k].astype(jnp.float32) for k in range(8)], axis=1)
        normed_in[...] = norm_rows(x_in[...], ffn_gain[...]).astype(jnp.bfloat16)
        total[...] = jnp.zeros_like(total)

    up = w[0, 0, :, :, :, 0:80, :].reshape(1280, 640)
    down = w[0, 0, :, :, :, 80:160, :].reshape(1280, 640)
    pre = jnp.dot(normed_in[...], up, preferred_element_type=jnp.float32)
    hidden = (pre / (1.0 + jnp.exp(-pre))).astype(jnp.bfloat16)
    total[...] += lax.dot_general(hidden, down, NT, preferred_element_type=jnp.float32)

    @pl.when(step == 7)
    def _():
        residual = x_in[...] + 0.5 * total[...]
        normed = norm_rows(residual, final_gain[...]).astype(jnp.bfloat16)
        logits = jnp.dot(normed, ctc[...], preferred_element_type=jnp.float32)
        shifted = logits - jnp.max(logits, axis=-1, keepdims=True)
        out = shifted - jnp.log(jnp.sum(jnp.exp(shifted), axis=-1, keepdims=True))
        emis[...] = out
        transfer[...] = viterbi(scal, out, ids[...], states)


def local_part(scal, w, mine, ffn_gain, final_gain, ctc, ids):
    whole = lambda *dims: pl.BlockSpec(dims, lambda i, s: (0,) * len(dims))
    return pl.pallas_call(
        local_kernel,
        out_shape=(jax.ShapeDtypeStruct((256, 256), jnp.float32), jax.ShapeDtypeStruct((128, 128), jnp.float32)),
        grid_spec=pltpu.PrefetchScalarGridSpec(
            num_scalar_prefetch=1,
            grid=(8,),
            in_specs=[
                pl.BlockSpec((1, 1, 2, 4, 2, 160, 640), lambda i, s: (i // 2, i % 2, 0, 0, 0, 0, 0)),
                whole(8, 256, 160), whole(1, 1280), whole(1, 1280), whole(1280, 256), whole(128, 2),
            ],
            out_specs=(whole(256, 256), whole(128, 128)),
            scratch_shapes=[
                pltpu.VMEM((256, 1280), jnp.float32),
                pltpu.VMEM((256, 1280), jnp.bfloat16),
                pltpu.VMEM((256, 1280), jnp.float32),
                pltpu.VMEM((400, 128), jnp.float32),
            ],
        ),
        compiler_params=pltpu.CompilerParams(vmem_limit_bytes=40 * MIB, dimension_semantics=("arbitrary",)),
        name="local_part",
    )(scal, w, mine, ffn_gain, final_gain, ctc, ids)


def row_to_column(row):
    i = lax.broadcasted_iota(jnp.int32, (128, 128), 0)
    j = lax.broadcasted_iota(jnp.int32, (128, 128), 1)
    return jnp.max(jnp.where(i == j, jnp.broadcast_to(row, (128, 128)), 4 * NEG), axis=1, keepdims=True)


def advance(column, matrix):
    return jnp.max(column + matrix, axis=0, keepdims=True)


def prefix_kernel(transfer, out, group, rows, spans, entry, entries, ts, tr, ps, pr, es, er, local_sem):
    tm, chan = lax.axis_index("tm"), lax.axis_index("chan")
    root = tm == 0
    barrier = pltpu.get_barrier_semaphore()
    for d in range(1, 8):
        pl.semaphore_signal(barrier, inc=1, device_id=(tm, lax.rem(chan + d, 8)), device_id_type=MESH)

    @pl.when(root)
    def _():
        def greet(k, carry):
            g, c = k // 8, lax.rem(k, 8)

            @pl.when(jnp.logical_or(g != tm, c != chan))
            def _():
                pl.semaphore_signal(barrier, inc=1, device_id=(g, c), device_id_type=MESH)

            return carry

        lax.fori_loop(0, 128, greet, 0)
        pl.semaphore_wait(barrier, 7 + 7 + 15)

    @pl.when(jnp.logical_not(root))
    def _():
        pl.semaphore_signal(barrier, inc=1, device_id=(0, chan), device_id_type=MESH)
        pl.semaphore_wait(barrier, 7 + 8)

    copies = []
    for d in range(1, 8):
        copy = pltpu.make_async_remote_copy(
            src_ref=transfer, dst_ref=group.at[chan], send_sem=ts.at[d - 1], recv_sem=tr.at[d - 1],
            device_id=(tm, lax.rem(chan + d, 8)), device_id_type=MESH,
        )
        copy.start()
        copies.append(copy)
    group[chan] = transfer[...]
    for copy in copies:
        copy.wait()

    span = group[0, pl.ds(pl.multiple_of(chan * 16, 16), 16), :]

    def grow(m, span):
        best = span[:, 0:1] + group[m, 0:1, :]
        for i in range(1, 128):
            best = jnp.maximum(best, span[:, i : i + 1] + group[m, i : i + 1, :])
        return best

    rows[...] = lax.fori_loop(1, 8, grow, span)

    mine = spans.at[tm, pl.ds(pl.multiple_of(chan * 16, 16), 16), :]
    for c in range(8):
        copy = pltpu.make_async_remote_copy(
            src_ref=rows, dst_ref=mine, send_sem=ps.at[c], recv_sem=pr.at[tm, chan],
            device_id=(0, c), device_id_type=MESH,
        )

        @pl.when(jnp.logical_not(jnp.logical_and(root, chan == c)))
        def _():
            copy.start()

        @pl.when(jnp.logical_and(root, chan == c))
        def _():
            same = pltpu.make_async_copy(rows, mine, local_sem)
            same.start()
            same.wait()

    @pl.when(root)
    def _():
        def await_rows(k, carry):
            g, c = k // 8, lax.rem(k, 8)
            here = spans.at[g, pl.ds(pl.multiple_of(c * 16, 16), 16), :]

            @pl.when(jnp.logical_or(g != tm, c != chan))
            def _():
                pltpu.make_async_copy(here, here, pr.at[g, c]).wait()

            return carry

        row = jnp.zeros((1, 128), jnp.float32)
        entry[...] = jnp.broadcast_to(row, (8, 128))
        lax.fori_loop(0, 128, await_rows, 0)

        def chain(g, row):
            row = advance(row_to_column(row), spans[g])
            entries[g] = jnp.broadcast_to(row, (8, 128))
            copy = pltpu.make_async_remote_copy(
                src_ref=entries.at[g], dst_ref=entry, send_sem=es.at[g], recv_sem=er,
                device_id=(g + 1, chan), device_id_type=MESH,
            )
            copy.start()
            return row

        lax.fori_loop(0, 15, chain, row)

        def sent(g, carry):
            pltpu.make_async_copy(entries.at[g], entries.at[g], es.at[g]).wait()
            return carry

        lax.fori_loop(0, 15, sent, 0)

    @pl.when(jnp.logical_not(root))
    def _():
        pltpu.make_async_copy(entry, entry, er).wait()

    row = lax.fori_loop(0, chan + 1, lambda m, row: advance(row_to_column(row), group[m]), entry[0:1, :])
    out[...] = jnp.where(row > 0.5 * NEG, row * (1.0 / 32768), 0.0)
    for c in range(8):

        @pl.when(jnp.logical_not(jnp.logical_and(root, chan == c)))
        def _():
            pltpu.make_async_copy(rows, rows, ps.at[c]).wait()


def prefix(transfer):
    dma = pltpu.SemaphoreType.DMA
    return pl.pallas_call(
        prefix_kernel,
        out_shape=jax.ShapeDtypeStruct((1, 128), jnp.float32),
        in_specs=[VM],
        out_specs=VM,
        scratch_shapes=[
            pltpu.VMEM((8, 128, 128), jnp.float32),
            pltpu.VMEM((16, 128), jnp.float32),
            pltpu.VMEM((16, 128, 128), jnp.float32),
            pltpu.VMEM((8, 128), jnp.float32),
            pltpu.VMEM((16, 8, 128), jnp.float32),
            dma((7,)), dma((7,)), dma((8,)), dma((16, 8)), dma((16,)), dma, dma,
        ],
        compiler_params=pltpu.CompilerParams(collective_id=2, has_side_effects=True),
        name="prefix",
    )(transfer)


def window_facts(labels, starts, widths):
    shard = lax.axis_index("tm") * 8 + lax.axis_index("chan")
    prior = jnp.maximum(shard - 1, 0)
    start_in = jnp.where(shard > 0, starts[prior], 0)
    width_in = jnp.where(shard > 0, widths[prior], 2)
    par = lax.rem(start_in, 2)
    base = start_in - par
    window = lax.dynamic_slice_in_dim(labels, base, 256)
    odd = window.reshape(128, 2)[:, 1]
    before = jnp.concatenate([jnp.full((1,), -1, jnp.int32), odd[:-1]])
    ids = jnp.stack([odd, before], axis=1).reshape(8, 16, 2).transpose(1, 0, 2).reshape(128, 2)
    scal = jnp.stack([par, width_in, starts[shard] - start_in, widths[shard]]).astype(jnp.int32)
    return scal, ids


def local(frames, up_weight, down_weight, ffn_gain, final_gain, ctc_weight, labels, starts, widths):
    scal, ids = window_facts(labels, starts, widths)
    chunk = jnp.concatenate([up_weight, down_weight.T], axis=0)
    w, mine = gather(frames, chunk)
    emissions, transfer = local_part(scal, w, mine, ffn_gain[None, :], final_gain[None, :], ctc_weight, ids)
    return emissions, prefix(transfer)


def solution(mesh):
    in_specs = (P("tm", "chan"), P("tm", "chan"), P("chan", "tm"), P(), P(), P(), P(), P(), P())
    out_specs = (P(("tm", "chan"), None), P(("tm", "chan"), None))
    return jax.shard_map(local, mesh=mesh, in_specs=in_specs, out_specs=out_specs, check_vma=False)
```

```python
import functools

import jax
import jax.numpy as jnp
from jax import lax
from jax.experimental import pallas as pl
from jax.experimental.pallas import tpu as pltpu
from jax.sharding import PartitionSpec as P

BAND = 128
LN_EPSILON = 1e-05
NEG = -1e30
MESH = pl.DeviceIdType.MESH
ANY = pl.BlockSpec(memory_space=pl.ANY)
VM = pl.BlockSpec(memory_space=pltpu.VMEM)
MIB = 2**20


def position():
    tm, chan = lax.axis_index("tm"), lax.axis_index("chan")
    x = lax.rem(chan, 2) * 2 + tm // 8
    return x, lax.rem(tm // 2, 4), chan // 2, lax.rem(tm, 2)


def device(x, y, z, core):
    return (lax.rem(x, 2) * 8 + y * 2 + core, z * 2 + x // 2)


def moved(pos, axis, by):
    out = list(pos)
    out[axis] = lax.rem(pos[axis] + by + 4, 4)
    return tuple(out)


PARTS = ((0, 64, (2, 0, 1)), (64, 48, (1, 2, 0)), (112, 48, (0, 1, 2)))
STEPS = (0, -1, 1, 2)
NT = (((1,), (1,)), ((), ()))


def block_at(w, pos, part):
    x, y, z, core = pos
    row, rows, _ = part
    return w.at[z, x // 2, lax.rem(x, 2), y, core, pl.ds(row, rows)]


def column_at(w, pos, part):
    x, y, z, core = pos
    row, rows, (axis, _, _) = part
    if axis == 0:
        return w.at[z, :, :, y, core, pl.ds(row, rows)]
    if axis == 1:
        return w.at[z, x // 2, lax.rem(x, 2), :, core, pl.ds(row, rows)]
    return w.at[:, x // 2, lax.rem(x, 2), y, core, pl.ds(row, rows)]


def norm_rows(values, gain_row):
    row_mean = jnp.mean(values, axis=-1, keepdims=True)
    centred = values - row_mean
    row_var = jnp.mean(jnp.square(centred), axis=-1, keepdims=True)
    return centred * lax.rsqrt(row_var + LN_EPSILON) * gain_row


def gain_row(ref):
    return jnp.concatenate([ref[k : k + 1, :] for k in range(10)], axis=1)


def block_kernel(
    frames, up, down, ffn_gain, final_gain, ctc_hbm, emis,
    w, mine, ctc, x_in, normed_in, total,
    local_sem, fr_send, fr_recv, s1, r1, s2, r2, s0, r0, s3, r3, sc, rc,
):
    me = position()
    x, y, z, core = me
    tm, chan = lax.axis_index("tm"), lax.axis_index("chan")
    sibling = (tm + 1 - 2 * core, chan)

    barrier = pltpu.get_barrier_semaphore()
    for axis in range(3):
        for by in (1, -1):
            pl.semaphore_signal(barrier, inc=1, device_id=device(*moved(me, axis, by)), device_id_type=MESH)
    pl.semaphore_signal(barrier, inc=1, device_id=sibling, device_id_type=MESH)
    for d in range(1, 8):
        pl.semaphore_signal(barrier, inc=1, device_id=(tm, lax.rem(chan + d, 8)), device_id_type=MESH)
    here = w.at[z, x // 2, lax.rem(x, 2), y, core]
    locals_ = [
        pltpu.make_async_copy(up, here.at[pl.ds(0, 80)], local_sem.at[0]),
        pltpu.make_async_copy(down, here.at[pl.ds(80, 80)], local_sem.at[1]),
        pltpu.make_async_copy(frames.at[:, pl.ds(pl.multiple_of(chan * 256, 256), 256)], mine.at[chan], local_sem.at[2]),
        pltpu.make_async_copy(ctc_hbm, ctc, local_sem.at[3]),
    ]
    for copy in locals_:
        copy.start()
    locals_[0].wait()
    locals_[1].wait()
    pl.semaphore_wait(barrier, 14)

    pending = []

    def send(ref, send_sem, recv_sem, to, dst=None):
        copy = pltpu.make_async_remote_copy(
            src_ref=ref, dst_ref=ref if dst is None else dst, send_sem=send_sem, recv_sem=recv_sem,
            device_id=to, device_id_type=MESH,
        )
        copy.start()
        pending.append(copy)

    def arrived(ref, sem):
        pltpu.make_async_copy(ref, ref, sem).wait()

    def both_ways(ref, axis, send_sems, recv_sems):
        send(ref, send_sems(0), recv_sems(1), device(*moved(me, axis, 1)))
        send(ref, send_sems(1), recv_sems(2), device(*moved(me, axis, -1)))

    def to_sibling(p, k, ref):
        send(ref, sc.at[p, k], rc.at[p, k], sibling)

    for p, part in enumerate(PARTS):
        both_ways(block_at(w, me, part), part[2][0], lambda k: s1.at[p, k], lambda k: r1.at[p, k])
    for d in range(1, 8):
        peer = lax.rem(chan + d, 8)
        send(
            frames.at[:, pl.ds(pl.multiple_of(peer * 256, 256), 256)], fr_send.at[d - 1], fr_recv.at[d - 1],
            (tm, peer), mine.at[chan],
        )
    for p, part in enumerate(PARTS):
        both_ways(block_at(w, me, part), part[2][1], lambda k: s2.at[p, 0, k], lambda k: r2.at[p, 0, k])
    for p, part in enumerate(PARTS):
        both_ways(block_at(w, me, part), part[2][2], lambda k: s0.at[p, 0, k], lambda k: r0.at[p, 0, k])
    for k in (1, 2, 3):
        for p, part in enumerate(PARTS):
            a, b, c = part[2]
            block = block_at(w, moved(me, a, STEPS[k]), part)
            arrived(block, r1.at[p, k])
            if k == 1 + p % 2:
                send(block, s1.at[p, 2], r1.at[p, 3], device(*moved(me, a, -STEPS[k])))
            both_ways(block, b, lambda q: s2.at[p, k, q], lambda q: r2.at[p, k, q])
            both_ways(block, c, lambda q: s0.at[p, k, q], lambda q: r0.at[p, k, q])
    for p, part in enumerate(PARTS):
        to_sibling(p, 0, column_at(w, me, part))

    def second(j):
        for p, part in enumerate(PARTS):
            a, b, c = part[2]
            for k in range(4):
                block = block_at(w, moved(moved(me, b, STEPS[j]), a, STEPS[k]), part)
                arrived(block, r2.at[p, k, j])
                if j == 1 + k % 2:
                    send(block, s2.at[p, k, 2], r2.at[p, k, 3], device(*moved(me, b, -STEPS[j])))
            column = column_at(w, moved(me, b, STEPS[j]), part)
            both_ways(column, c, lambda q: s3.at[p, j, q], lambda q: r3.at[p, j, q])
            to_sibling(p, j, column)

    def third(i, j, p):
        part = PARTS[p]
        a, b, c = part[2]
        at = moved(moved(me, c, STEPS[i]), b, STEPS[j])
        column = column_at(w, at, part)
        if j == 0 and i < 3:
            for k in range(4):
                arrived(block_at(w, moved(at, a, STEPS[k]), part), r0.at[p, k, i])
        else:
            arrived(column, r3.at[p, j, i])
        if i == 1 + j % 2:
            send(column, s3.at[p, j, 2], r3.at[p, j, 3], device(*moved(me, c, -STEPS[i])))
        to_sibling(p, 4 * i + j, column)

    other = (x, y, z, 1 - core)

    def from_sibling(i, j, p):
        _, b, c = PARTS[p][2]
        arrived(column_at(w, moved(moved(other, c, STEPS[i]), b, STEPS[j]), PARTS[p]), rc.at[p, 4 * i + j])

    second(1)
    for i in (1, 2):
        for p in range(3):
            third(i, 0, p)

    locals_[2].wait()
    for d in range(1, 8):
        arrived(mine.at[lax.rem(chan + 8 - d, 8)], fr_recv.at[d - 1])
    x_in[...] = jnp.transpose(mine[...].astype(jnp.float32).reshape(1280, 256))
    normed_in[...] = norm_rows(x_in[...], gain_row(ffn_gain)).astype(jnp.bfloat16)
    total[...] = jnp.zeros_like(total)

    second(2)
    second(3)
    for j in (1, 2, 3):
        for i in (1, 2):
            for p in range(3):
                third(i, j, p)

    def ffn(zz, xx):
        up_all = w[zz, xx, :, :, :, 0:80, :].reshape(1280, 640)
        down_all = w[zz, xx, :, :, :, 80:160, :].reshape(1280, 640)
        pre = jnp.dot(normed_in[...], up_all, preferred_element_type=jnp.float32)
        hidden = (pre / (1.0 + jnp.exp(-pre))).astype(jnp.bfloat16)
        total[...] += lax.dot_general(hidden, down_all, NT, preferred_element_type=jnp.float32)

    def ffn_loop(first, count, xx):
        def one(q, carry):
            ffn(lax.rem(z + q, 4), xx)
            return carry

        lax.fori_loop(first, first + count, one, 0)

    for j in (0, 1, 2):
        third(3, j, 0)
    for i in range(3):
        for j in range(4):
            for p in range(3):
                from_sibling(i, j, p)
    for j in (0, 1, 2):
        from_sibling(3, j, 0)
    ffn_loop(3, 3, x // 2)
    for j in range(4):
        third(3, j, 2)
    third(3, 3, 0)
    for j in range(4):
        third(3, j, 1)
    for j in range(4):
        from_sibling(3, j, 2)
    ffn_loop(2, 1, x // 2)
    from_sibling(3, 3, 0)
    for j in range(4):
        from_sibling(3, j, 1)
    ffn_loop(0, 4, 1 - x // 2)

    locals_[3].wait()
    residual = x_in[...] + 0.5 * total[...]
    normed = norm_rows(residual, gain_row(final_gain)).astype(jnp.bfloat16)
    logits = jnp.dot(normed, ctc[...], preferred_element_type=jnp.float32)
    shifted = logits - jnp.max(logits, axis=-1, keepdims=True)
    emis[...] = shifted - jnp.log(jnp.sum(jnp.exp(shifted), axis=-1, keepdims=True))
    for copy in pending:
        copy.wait_send()


def block_part(frames, up, down, ffn_gain, final_gain, ctc):
    dma = pltpu.SemaphoreType.DMA
    return pl.pallas_call(
        block_kernel,
        out_shape=jax.ShapeDtypeStruct((256, 256), jnp.float32),
        in_specs=[ANY, ANY, ANY, VM, VM, ANY],
        out_specs=VM,
        scratch_shapes=[
            pltpu.VMEM((4, 2, 2, 4, 2, 160, 640), jnp.bfloat16),
            pltpu.VMEM((8, 160, 256), jnp.bfloat16),
            pltpu.VMEM((1280, 256), jnp.bfloat16),
            pltpu.VMEM((256, 1280), jnp.float32),
            pltpu.VMEM((256, 1280), jnp.bfloat16),
            pltpu.VMEM((256, 1280), jnp.float32),
            dma((4,)), dma((7,)), dma((7,)),
            dma((3, 3)), dma((3, 4)),
            dma((3, 4, 3)), dma((3, 4, 4)),
            dma((3, 4, 2)), dma((3, 4, 3)),
            dma((3, 4, 3)), dma((3, 4, 4)),
            dma((3, 16)), dma((3, 16)),
        ],
        compiler_params=pltpu.CompilerParams(collective_id=1, has_side_effects=True, vmem_limit_bytes=52 * MIB),
        name="block",
    )(frames, up, down, ffn_gain, final_gain, ctc)


def split(values):
    high = values.astype(jnp.bfloat16)
    return high, (values - high.astype(jnp.float32)).astype(jnp.bfloat16)


def state_ids(labels, base):
    row0 = jnp.minimum(base // 128, 61)
    window = jnp.concatenate([labels[pl.ds(row0 + k, 1), :] for k in range(3)], axis=1)
    r = lax.broadcasted_iota(jnp.int32, (128, 384), 0)
    lane = lax.broadcasted_iota(jnp.int32, (128, 384), 1)
    at = base - row0 * 128 + 2 * ((r % 8) * 16 + r // 8) + 1
    pick = lambda here: jnp.sum(jnp.where(lane == here, window, 0), axis=1, keepdims=True)
    return pick(at), pick(at - 2)


def transfer_matrix(emissions, labels, start_in, width_in, start_out, width_out, states):
    par = lax.rem(start_in, 2)
    offset = start_out - start_in
    ids, ids_before = state_ids(labels, start_in - par)
    char = lax.broadcasted_iota(jnp.int32, (128, 256), 1)
    choose = ((ids == char).astype(jnp.float32) - (char == 0).astype(jnp.float32)).astype(jnp.bfloat16)
    high, low = split(emissions)
    rest = (emissions - high.astype(jnp.float32) - low.astype(jnp.float32)).astype(jnp.bfloat16)
    gain = sum(lax.dot_general(choose, part, NT, preferred_element_type=jnp.float32) for part in (high, low, rest))
    blank = jnp.sum(emissions[:, 0:1])
    skip = jnp.broadcast_to(jnp.where(ids == ids_before, NEG, 0.0), (128, 128)).reshape(16, 8, 128)
    v = lax.broadcasted_iota(jnp.int32, (16, 8, 128), 0)
    sub = lax.broadcasted_iota(jnp.int32, (16, 8, 128), 1)
    start = lax.broadcasted_iota(jnp.int32, (16, 8, 128), 2)
    at = 2 * (sub * 16 + v) - par
    live = start < width_in
    even = jnp.where((at == start) & live, 0.0, NEG)
    odd = jnp.where((at + 1 == start) & live, 0.0, NEG)
    top = jnp.full((8, 128), NEG, jnp.float32)
    first = lax.broadcasted_iota(jnp.int32, (8, 128), 0) == 0
    for half in range(2):
        block = gain[:, half * 128 : half * 128 + 128].reshape(16, 8, 128)
        for t in range(128):
            step = jnp.broadcast_to(block[:, :, t : t + 1], (16, 8, 128))
            turned = pltpu.roll(odd[15], 1, 0)
            below = jnp.concatenate([jnp.where(first, NEG, turned)[None], odd[:15]], axis=0)
            top = jnp.maximum(top, turned)
            odd = jnp.maximum(jnp.maximum(odd, even), below + skip) + step
            even = jnp.maximum(even, below)
    for k in range(16):
        states[pl.ds(2 * k, 8, stride=32), :] = even[k]
        states[pl.ds(2 * k + 1, 8, stride=32), :] = odd[k]
    states[256:264, :] = top
    reached = states[pl.ds(par + offset, 128), :]
    row = lax.broadcasted_iota(jnp.int32, (128, 128), 0)
    reached = jnp.where(row < width_out, reached + blank, NEG)
    return jnp.transpose(reached)


def row_to_column(row):
    i = lax.broadcasted_iota(jnp.int32, (128, 128), 0)
    j = lax.broadcasted_iota(jnp.int32, (128, 128), 1)
    return jnp.max(jnp.where(i == j, jnp.broadcast_to(row, (128, 128)), 4 * NEG), axis=1, keepdims=True)


def advance(column, matrix):
    return jnp.max(column + matrix, axis=0, keepdims=True)


def path_kernel(
    starts, widths, labels, emissions, out, states, transfer, group, rows, spans, entry, entries,
    ts, tr, ps, pr, es, er,
):
    tm, chan = lax.axis_index("tm"), lax.axis_index("chan")
    root = tm == 0
    barrier = pltpu.get_barrier_semaphore()
    for d in range(1, 8):
        pl.semaphore_signal(barrier, inc=1, device_id=(tm, lax.rem(chan + d, 8)), device_id_type=MESH)

    @pl.when(root)
    def _():
        def greet(g, carry):
            for d in range(8):

                @pl.when(jnp.logical_or(g != 0, d != 0))
                def _():
                    pl.semaphore_signal(barrier, inc=1, device_id=(g, lax.rem(chan + d, 8)), device_id_type=MESH)

            return carry

        lax.fori_loop(0, 16, greet, 0)

    @pl.when(jnp.logical_not(root))
    def _():
        pl.semaphore_signal(barrier, inc=1, device_id=(0, chan), device_id_type=MESH)

    shard = tm * 8 + chan
    prior = jnp.maximum(shard - 1, 0)
    start_in = jnp.where(shard > 0, starts[prior], 0)
    width_in = jnp.where(shard > 0, widths[prior], 2)
    transfer[...] = transfer_matrix(
        emissions[...], labels, start_in, width_in, starts[shard], widths[shard], states
    )

    @pl.when(root)
    def _():
        pl.semaphore_wait(barrier, 7 + 7 + 15)

    @pl.when(jnp.logical_not(root))
    def _():
        pl.semaphore_wait(barrier, 7 + 8)

    copies = []
    for d in range(1, 8):
        copy = pltpu.make_async_remote_copy(
            src_ref=transfer, dst_ref=group.at[chan], send_sem=ts.at[d - 1], recv_sem=tr.at[d - 1],
            device_id=(tm, lax.rem(chan + d, 8)), device_id_type=MESH,
        )
        copy.start()
        copies.append(copy)
    group[chan] = transfer[...]
    for copy in copies:
        copy.wait_recv()

    span = group[0, pl.ds(pl.multiple_of(chan * 16, 16), 16), :]

    def grow(m, span):
        best = span[:, 0:1] + group[m, 0:1, :]
        for i in range(1, 128):
            best = jnp.maximum(best, span[:, i : i + 1] + group[m, i : i + 1, :])
        return best

    rows[...] = lax.fori_loop(1, 8, grow, span)
    for copy in copies:
        copy.wait_send()

    at = pl.ds(pl.multiple_of(tm * 128 + chan * 16, 16), 16)
    for c in range(8):

        @pl.when(jnp.logical_not(jnp.logical_and(root, chan == c)))
        def _():
            pltpu.make_async_remote_copy(
                src_ref=rows, dst_ref=spans.at[at], send_sem=ps.at[c], recv_sem=pr,
                device_id=(0, c), device_id_type=MESH,
            ).start()

    @pl.when(root)
    def _():
        spans[at, :] = rows[...]
        row = jnp.zeros((1, 128), jnp.float32)
        entry[...] = jnp.broadcast_to(row, (8, 128))
        others = spans.at[pl.ds(0, 127 * 16)]
        pltpu.make_async_copy(others, others, pr).wait()

        def chain(g, row):
            row = advance(row_to_column(row), spans[pl.ds(pl.multiple_of(g * 128, 128), 128), :])
            entries[g] = jnp.broadcast_to(row, (8, 128))
            pltpu.make_async_remote_copy(
                src_ref=entries.at[g], dst_ref=entry, send_sem=es.at[g], recv_sem=er,
                device_id=(g + 1, chan), device_id_type=MESH,
            ).start()
            return row

        lax.fori_loop(0, 15, chain, row)

    @pl.when(jnp.logical_not(root))
    def _():
        pltpu.make_async_copy(entry, entry, er).wait()

    row = lax.fori_loop(0, chan + 1, lambda m, row: advance(row_to_column(row), group[m]), entry[0:1, :])
    out[...] = jnp.where(row > 0.5 * NEG, row * (1.0 / 32768), 0.0)

    @pl.when(root)
    def _():
        def sent(g, carry):
            pltpu.make_async_copy(entries.at[g], entries.at[g], es.at[g]).wait()
            return carry

        lax.fori_loop(0, 15, sent, 0)

    for c in range(8):

        @pl.when(jnp.logical_not(jnp.logical_and(root, chan == c)))
        def _():
            pltpu.make_async_copy(rows, rows, ps.at[c]).wait()


def path_part(starts, widths, labels, emissions):
    dma = pltpu.SemaphoreType.DMA
    smem = pl.BlockSpec(memory_space=pltpu.SMEM)
    return pl.pallas_call(
        path_kernel,
        out_shape=jax.ShapeDtypeStruct((1, 128), jnp.float32),
        in_specs=[smem, smem, VM, VM],
        out_specs=VM,
        scratch_shapes=[
            pltpu.VMEM((264, 128), jnp.float32),
            pltpu.VMEM((128, 128), jnp.float32),
            pltpu.VMEM((8, 128, 128), jnp.float32),
            pltpu.VMEM((16, 128), jnp.float32),
            pltpu.VMEM((2048, 128), jnp.float32),
            pltpu.VMEM((8, 128), jnp.float32),
            pltpu.VMEM((16, 8, 128), jnp.float32),
            dma((7,)), dma((7,)), dma((8,)), dma, dma((16,)), dma,
        ],
        compiler_params=pltpu.CompilerParams(collective_id=2, has_side_effects=True, vmem_limit_bytes=24 * MIB),
        name="path",
    )(starts, widths, labels, emissions)


def local(frames, up_weight, down_weight, ffn_gain, final_gain, ctc_weight, labels, starts, widths):
    emissions = block_part(
        frames.T, up_weight, down_weight.T, ffn_gain.reshape(10, 128), final_gain.reshape(10, 128), ctc_weight
    )
    return emissions, path_part(starts, widths, labels.reshape(64, 128), emissions)


def solution(mesh):
    in_specs = (P("tm", "chan"), P("tm", "chan"), P("chan", "tm"), P(), P(), P(), P(), P(), P())
    out_specs = (P(("tm", "chan"), None), P(("tm", "chan"), None))
    return jax.shard_map(local, mesh=mesh, in_specs=in_specs, out_specs=out_specs, check_vma=False)
```

```python
import functools

import jax
import jax.numpy as jnp
from jax import lax
from jax.experimental import pallas as pl
from jax.experimental.pallas import tpu as pltpu
from jax.sharding import PartitionSpec as P

BAND = 128
LN_EPSILON = 1e-05
NEG = -1e30
MESH = pl.DeviceIdType.MESH
ANY = pl.BlockSpec(memory_space=pl.ANY)
HBM = pl.BlockSpec(memory_space=pltpu.HBM)
VM = pl.BlockSpec(memory_space=pltpu.VMEM)
MIB = 2**20


def position():
    tm, chan = lax.axis_index("tm"), lax.axis_index("chan")
    x = lax.rem(chan, 2) * 2 + tm // 8
    return x, lax.rem(tm // 2, 4), chan // 2, lax.rem(tm, 2)


def device(x, y, z, core):
    return (lax.rem(x, 2) * 8 + y * 2 + core, z * 2 + x // 2)


def moved(pos, axis, by):
    out = list(pos)
    out[axis] = lax.rem(pos[axis] + by + 4, 4)
    return tuple(out)


PARTS = (
    (0, 64, (2, 0, 1)), (64, 48, (1, 2, 0)), (112, 48, (0, 1, 2)),
)
ALL = (0, 1, 2)
ORDER = (
    (0, 0, 1), (0, 0, 2), (0, 1, 1), (0, 1, 2), (0, 2, 1), (0, 2, 2), (1, 0, 0, 1), (1, 0, 0, 2), (1, 1, 0, 1),
    (1, 1, 0, 2), (1, 2, 0, 1), (1, 2, 0, 2), (7, 0, 1), (3, 0, 1), (1, 0, 1, 1), (1, 0, 1, 2), (7, 1, 1),
    (1, 1, 1, 1), (1, 1, 1, 2), (7, 2, 1), (3, 2, 1), (1, 2, 1, 1), (1, 2, 1, 2), (7, 0, 2), (1, 0, 2, 1),
    (1, 0, 2, 2), (7, 1, 2), (3, 1, 2), (1, 1, 2, 1), (1, 1, 2, 2), (7, 2, 2), (1, 2, 2, 1), (1, 2, 2, 2),
    (7, 0, 3), (1, 0, 3, 1), (1, 0, 3, 2), (7, 1, 3), (1, 1, 3, 1), (1, 1, 3, 2), (7, 2, 3), (1, 2, 3, 1),
    (1, 2, 3, 2), (2, 0, 0, 1), (2, 0, 0, 2), (2, 1, 0, 1), (2, 1, 0, 2), (2, 2, 0, 1), (2, 2, 0, 2), (8, 0, 0, 1),
    (4, 0, 0, 1), (8, 0, 1, 1), (8, 0, 2, 1), (4, 0, 2, 1), (8, 0, 3, 1), (2, 0, 1, 1), (2, 0, 1, 2), (8, 1, 0, 1),
    (4, 1, 0, 1), (8, 1, 1, 1), (8, 1, 2, 1), (4, 1, 2, 1), (8, 1, 3, 1), (2, 1, 1, 1), (2, 1, 1, 2), (8, 2, 0, 1),
    (4, 2, 0, 1), (8, 2, 1, 1), (8, 2, 2, 1), (4, 2, 2, 1), (8, 2, 3, 1), (2, 2, 1, 1), (2, 2, 1, 2), (6,),
    (8, 0, 0, 2), (8, 0, 1, 2), (4, 0, 1, 2), (8, 0, 2, 2), (8, 0, 3, 2), (4, 0, 3, 2), (2, 0, 2, 1), (2, 0, 2, 2),
    (8, 1, 0, 2), (8, 1, 1, 2), (4, 1, 1, 2), (8, 1, 2, 2), (8, 1, 3, 2), (4, 1, 3, 2), (2, 1, 2, 1), (2, 1, 2, 2),
    (8, 2, 0, 2), (8, 2, 1, 2), (4, 2, 1, 2), (8, 2, 2, 2), (8, 2, 3, 2), (4, 2, 3, 2), (2, 2, 2, 1), (2, 2, 2, 2),
    (8, 0, 0, 3), (8, 0, 1, 3), (8, 0, 2, 3), (8, 0, 3, 3), (2, 0, 3, 1), (2, 0, 3, 2), (8, 1, 0, 3), (8, 1, 1, 3),
    (8, 1, 2, 3), (8, 1, 3, 3), (2, 1, 3, 1), (2, 1, 3, 2), (8, 2, 0, 3), (8, 2, 1, 3), (8, 2, 2, 3), (8, 2, 3, 3),
    (2, 2, 3, 1), (2, 2, 3, 2), (9, 0, 0, 1), (5, 0, 0, 1), (9, 1, 0, 1), (5, 1, 0, 1), (9, 2, 0, 1), (5, 2, 0, 1),
    (9, 0, 1, 1), (9, 1, 1, 1), (9, 2, 1, 1), (9, 0, 2, 1), (5, 0, 2, 1), (9, 1, 2, 1), (5, 1, 2, 1), (9, 2, 2, 1),
    (5, 2, 2, 1), (9, 0, 3, 1), (9, 1, 3, 1), (9, 2, 3, 1), (10,), (9, 0, 0, 2), (9, 1, 0, 2), (9, 2, 0, 2),
    (9, 0, 1, 2), (5, 0, 1, 2), (9, 1, 1, 2), (5, 1, 1, 2), (9, 2, 1, 2), (5, 2, 1, 2), (9, 0, 2, 2), (9, 1, 2, 2),
    (9, 2, 2, 2), (9, 0, 3, 2), (5, 0, 3, 2), (9, 1, 3, 2), (5, 1, 3, 2), (9, 2, 3, 2), (5, 2, 3, 2), (9, 0, 0, 3),
    (9, 0, 1, 3), (9, 0, 2, 3), (9, 2, 0, 3), (9, 2, 1, 3), (9, 2, 2, 3), (9, 2, 3, 3), (9, 0, 3, 3), (9, 1, 0, 3),
    (9, 1, 1, 3), (9, 1, 2, 3), (9, 1, 3, 3),
)
STEPS = (0, -1, 1, 2)
NT = (((1,), (1,)), ((), ()))


def block_at(w, pos, part):
    x, y, z, core = pos
    row, rows, _ = part
    return w.at[z, x // 2, lax.rem(x, 2), y, core, pl.ds(row, rows)]


def column_at(w, pos, part):
    x, y, z, core = pos
    row, rows, (axis, _, _) = part
    if axis == 0:
        return w.at[z, :, :, y, core, pl.ds(row, rows)]
    if axis == 1:
        return w.at[z, x // 2, lax.rem(x, 2), :, core, pl.ds(row, rows)]
    return w.at[:, x // 2, lax.rem(x, 2), y, core, pl.ds(row, rows)]


def slab_at(w, pos, part):
    x, y, z, core = pos
    row, rows, (_, _, axis) = part
    if axis == 0:
        return w.at[:, x // 2, lax.rem(x, 2), :, core, pl.ds(row, rows)]
    if axis == 1:
        return w.at[:, :, :, y, core, pl.ds(row, rows)]
    return w.at[z, :, :, :, core, pl.ds(row, rows)]


def norm_rows(values, gain_row):
    row_mean = jnp.mean(values, axis=-1, keepdims=True)
    centred = values - row_mean
    row_var = jnp.mean(jnp.square(centred), axis=-1, keepdims=True)
    return centred * lax.rsqrt(row_var + LN_EPSILON) * gain_row


def gain_row(ref):
    return jnp.concatenate([ref[k : k + 1, :] for k in range(10)], axis=1)


def block_kernel(
    frames, up, down, ffn_gain, final_gain, ctc_hbm, emis,
    w, mine, ctc, x_in, normed_in, total,
    local_sem, fr_send, fr_recv, s1, r1, s2, r2, s3, r3, sc, rc,
):
    me = position()
    x, y, z, core = me
    tm, chan = lax.axis_index("tm"), lax.axis_index("chan")
    sibling = (tm + 1 - 2 * core, chan)

    barrier = pltpu.get_barrier_semaphore()
    for axis in range(3):
        for by in (1, -1):
            pl.semaphore_signal(barrier, inc=1, device_id=device(*moved(me, axis, by)), device_id_type=MESH)
    pl.semaphore_signal(barrier, inc=1, device_id=sibling, device_id_type=MESH)
    for d in range(1, 8):
        pl.semaphore_signal(barrier, inc=1, device_id=(tm, lax.rem(chan + d, 8)), device_id_type=MESH)
    here = w.at[z, x // 2, lax.rem(x, 2), y, core]
    locals_ = [
        pltpu.make_async_copy(up, here.at[pl.ds(0, 80)], local_sem.at[0]),
        pltpu.make_async_copy(down, here.at[pl.ds(80, 80)], local_sem.at[1]),
        pltpu.make_async_copy(frames.at[:, pl.ds(pl.multiple_of(chan * 256, 256), 256)], mine.at[chan], local_sem.at[2]),
        pltpu.make_async_copy(ctc_hbm, ctc, local_sem.at[3]),
    ]
    for copy in locals_:
        copy.start()
    locals_[0].wait()
    locals_[1].wait()
    pl.semaphore_wait(barrier, 14)

    pending = []

    def send(ref, send_sem, recv_sem, to, dst=None):
        copy = pltpu.make_async_remote_copy(
            src_ref=ref, dst_ref=ref if dst is None else dst, send_sem=send_sem, recv_sem=recv_sem,
            device_id=to, device_id_type=MESH,
        )
        copy.start()
        pending.append(copy)

    def arrived(ref, sem):
        pltpu.make_async_copy(ref, ref, sem).wait()

    def both_ways(ref, axis, send_sems, recv_sems):
        send(ref, send_sems(0), recv_sems(1), device(*moved(me, axis, 1)))
        send(ref, send_sems(1), recv_sems(2), device(*moved(me, axis, -1)))

    def to_sibling(p, k, ref):
        send(ref, sc.at[p, k], rc.at[p, k], sibling)

    def step_to(pos, axis, place):
        return moved(pos, axis, STEPS[place])

    def send_to(ref, axis, q, send_sem, recv_sem):
        send(ref, send_sem, recv_sem, device(*moved(me, axis, 1 if q == 1 else -1)))

    arrivals = {}

    def count(key, full):
        arrivals[key] = arrivals.get(key, 0) + 1
        return arrivals[key] == full

    def communicate(event):
        kind, p, *at = event
        part = PARTS[p]
        a, b, c = part[2]
        if kind == 0:
            (q,) = at
            send_to(block_at(w, me, part), a, q, s1.at[p, q - 1], r1.at[p, q])
        elif kind == 1:
            k, q = at
            send_to(block_at(w, step_to(me, a, k), part), b, q, s2.at[p, k, q - 1], r2.at[p, k, q])
        elif kind == 2:
            j, q = at
            send_to(column_at(w, step_to(me, b, j), part), c, q, s3.at[p, j, q - 1], r3.at[p, j, q])
        elif kind == 3:
            (k,) = at
            send_to(block_at(w, step_to(me, a, k), part), a, k, s1.at[p, 2], r1.at[p, 3])
        elif kind == 4:
            k, j = at
            send_to(block_at(w, step_to(step_to(me, b, j), a, k), part), b, j, s2.at[p, k, 2], r2.at[p, k, 3])
        elif kind == 5:
            j, i = at
            send_to(column_at(w, step_to(step_to(me, c, i), b, j), part), c, i, s3.at[p, j, 2], r3.at[p, j, 3])
        elif kind == 7:
            (k,) = at
            arrived(block_at(w, step_to(me, a, k), part), r1.at[p, k])
            if count((p, 0), 15):
                to_sibling(p, 0, slab_at(w, me, part))
        elif kind == 8:
            k, j = at
            arrived(block_at(w, step_to(step_to(me, b, j), a, k), part), r2.at[p, k, j])
            if count((p, 0), 15):
                to_sibling(p, 0, slab_at(w, me, part))
        elif kind == 9:
            j, i = at
            there = step_to(step_to(me, c, i), b, j)
            column = column_at(w, there, part)
            arrived(column, r3.at[p, j, i])
            if i == 3:
                to_sibling(p, 3 + j, column)
            elif count((p, i), 4):
                to_sibling(p, i, slab_at(w, there, part))

    other = (x, y, z, 1 - core)

    def slab_from_sibling(i, p):
        c = PARTS[p][2][2]
        arrived(slab_at(w, moved(other, c, STEPS[i]), PARTS[p]), rc.at[p, i])

    def from_sibling(j, p):
        _, b, c = PARTS[p][2]
        arrived(column_at(w, moved(moved(other, c, 2), b, STEPS[j]), PARTS[p]), rc.at[p, 3 + j])

    def send_frames():
        for d in range(1, 8):
            peer = lax.rem(chan + d, 8)
            send(
                frames.at[:, pl.ds(pl.multiple_of(peer * 256, 256), 256)], fr_send.at[d - 1], fr_recv.at[d - 1],
                (tm, peer), mine.at[chan],
            )

    def norm_frames():
        locals_[2].wait()
        for d in range(1, 8):
            arrived(mine.at[lax.rem(chan + 8 - d, 8)], fr_recv.at[d - 1])
        x_in[...] = jnp.transpose(mine[...].astype(jnp.float32).reshape(1280, 256))
        normed_in[...] = norm_rows(x_in[...], gain_row(ffn_gain)).astype(jnp.bfloat16)
        total[...] = jnp.zeros_like(total)

    def project(first_step, count, xx):
        def one(q, carry):
            zz = lax.rem(z + q, 4)
            up_all = w[zz, xx, :, :, :, 0:80, :].reshape(1280, 640)
            down_all = w[zz, xx, :, :, :, 80:160, :].reshape(1280, 640)
            pre = jnp.dot(normed_in[...], up_all, preferred_element_type=jnp.float32)
            half = 0.5 * pre
            hidden = (half + half * jnp.tanh(half)).astype(jnp.bfloat16)
            total[...] += lax.dot_general(hidden, down_all, NT, preferred_element_type=jnp.float32)
            return carry

        lax.fori_loop(first_step, first_step + count, one, 0)

    for event in ORDER:
        if event[0] == 6:
            send_frames()
        elif event[0] == 10:
            norm_frames()
        else:
            communicate(event)
    on_y, on_x, on_z = ALL
    for p in ALL:
        for i in range(3):
            slab_from_sibling(i, p)
    for j in (0, 1, 2):
        from_sibling(j, on_y)
    project(3, 3, x // 2)
    for j in range(4):
        from_sibling(j, on_z)
    project(2, 1, x // 2)
    from_sibling(3, on_y)
    for j in range(4):
        from_sibling(j, on_x)
    project(0, 4, 1 - x // 2)

    locals_[3].wait()
    residual = x_in[...] + 0.5 * total[...]
    normed = norm_rows(residual, gain_row(final_gain)).astype(jnp.bfloat16)
    logits = jnp.dot(normed, ctc[...], preferred_element_type=jnp.float32)
    shifted = logits - jnp.max(logits, axis=-1, keepdims=True)
    emis[...] = shifted - jnp.log(jnp.sum(jnp.exp(shifted), axis=-1, keepdims=True))
    for copy in pending:
        copy.wait_send()


def block_part(frames, up, down, ffn_gain, final_gain, ctc):
    dma = pltpu.SemaphoreType.DMA
    return pl.pallas_call(
        block_kernel,
        out_shape=jax.ShapeDtypeStruct((256, 256), jnp.float32),
        in_specs=[HBM, HBM, HBM, VM, VM, HBM],
        out_specs=VM,
        scratch_shapes=[
            pltpu.VMEM((4, 2, 2, 4, 2, 160, 640), jnp.bfloat16),
            pltpu.VMEM((8, 160, 256), jnp.bfloat16),
            pltpu.VMEM((1280, 256), jnp.bfloat16),
            pltpu.VMEM((256, 1280), jnp.float32),
            pltpu.VMEM((256, 1280), jnp.bfloat16),
            pltpu.VMEM((256, 1280), jnp.float32),
            dma((4,)), dma((7,)), dma((7,)),
            dma((3, 3)), dma((3, 4)),
            dma((3, 4, 3)), dma((3, 4, 4)),
            dma((3, 4, 3)), dma((3, 4, 4)),
            dma((3, 7)), dma((3, 7)),
        ],
        compiler_params=pltpu.CompilerParams(collective_id=1, has_side_effects=True, vmem_limit_bytes=52 * MIB),
        name="block",
    )(frames, up, down, ffn_gain, final_gain, ctc)


def split(values):
    high = values.astype(jnp.bfloat16)
    return high, (values - high.astype(jnp.float32)).astype(jnp.bfloat16)


def state_ids(labels, base):
    row0 = jnp.minimum(base // 128, 61)
    window = jnp.concatenate([labels[pl.ds(row0 + k, 1), :] for k in range(3)], axis=1)
    r = lax.broadcasted_iota(jnp.int32, (128, 384), 0)
    lane = lax.broadcasted_iota(jnp.int32, (128, 384), 1)
    at = base - row0 * 128 + 2 * ((r % 8) * 16 + r // 8) + 1
    pick = lambda here: jnp.sum(jnp.where(lane == here, window, 0), axis=1, keepdims=True)
    return pick(at), pick(at - 2)


def transfer_matrix(emissions, labels, start_in, width_in, start_out, width_out, states):
    par = lax.rem(start_in, 2)
    offset = start_out - start_in
    ids, ids_before = state_ids(labels, start_in - par)
    char = lax.broadcasted_iota(jnp.int32, (128, 256), 1)
    choose = ((ids == char).astype(jnp.float32) - (char == 0).astype(jnp.float32)).astype(jnp.bfloat16)
    high, low = split(emissions)
    rest = (emissions - high.astype(jnp.float32) - low.astype(jnp.float32)).astype(jnp.bfloat16)
    gain = sum(lax.dot_general(choose, part, NT, preferred_element_type=jnp.float32) for part in (high, low, rest))
    blank = jnp.sum(emissions[:, 0:1])
    skip = jnp.broadcast_to(jnp.where(ids == ids_before, NEG, 0.0), (128, 128)).reshape(16, 8, 128)
    v = lax.broadcasted_iota(jnp.int32, (16, 8, 128), 0)
    sub = lax.broadcasted_iota(jnp.int32, (16, 8, 128), 1)
    start = lax.broadcasted_iota(jnp.int32, (16, 8, 128), 2)
    at = 2 * (sub * 16 + v) - par
    live = start < width_in
    even = jnp.where((at == start) & live, 0.0, NEG)
    odd = jnp.where((at + 1 == start) & live, 0.0, NEG)
    top = jnp.full((8, 128), NEG, jnp.float32)
    first = lax.broadcasted_iota(jnp.int32, (8, 128), 0) == 0
    for half in range(2):
        block = gain[:, half * 128 : half * 128 + 128].reshape(16, 8, 128)
        for t in range(128):
            step = jnp.broadcast_to(block[:, :, t : t + 1], (16, 8, 128))
            turned = pltpu.roll(odd[15], 1, 0)
            below = jnp.concatenate([jnp.where(first, NEG, turned)[None], odd[:15]], axis=0)
            top = jnp.maximum(top, turned)
            odd = jnp.maximum(jnp.maximum(odd, even), below + skip) + step
            even = jnp.maximum(even, below)
    for k in range(16):
        states[pl.ds(2 * k, 8, stride=32), :] = even[k]
        states[pl.ds(2 * k + 1, 8, stride=32), :] = odd[k]
    states[256:264, :] = top
    reached = states[pl.ds(par + offset, 128), :]
    row = lax.broadcasted_iota(jnp.int32, (128, 128), 0)
    reached = jnp.where(row < width_out, reached + blank, NEG)
    return jnp.transpose(reached)


def row_to_column(row):
    i = lax.broadcasted_iota(jnp.int32, (128, 128), 0)
    j = lax.broadcasted_iota(jnp.int32, (128, 128), 1)
    return jnp.max(jnp.where(i == j, jnp.broadcast_to(row, (128, 128)), 4 * NEG), axis=1, keepdims=True)


def advance(column, matrix):
    return jnp.max(column + matrix, axis=0, keepdims=True)


def path_kernel(
    starts, widths, labels, emissions, out, states, transfer, group, rows, spans, entry, entries,
    ts, tr, ps, pr, es, er,
):
    tm, chan = lax.axis_index("tm"), lax.axis_index("chan")
    root = tm == 0
    barrier = pltpu.get_barrier_semaphore()
    for d in range(1, 8):
        pl.semaphore_signal(barrier, inc=1, device_id=(tm, lax.rem(chan + d, 8)), device_id_type=MESH)

    @pl.when(root)
    def _():
        def greet(g, carry):
            for d in range(8):

                @pl.when(jnp.logical_or(g != 0, d != 0))
                def _():
                    pl.semaphore_signal(barrier, inc=1, device_id=(g, lax.rem(chan + d, 8)), device_id_type=MESH)

            return carry

        lax.fori_loop(0, 16, greet, 0)

    @pl.when(jnp.logical_not(root))
    def _():
        pl.semaphore_signal(barrier, inc=1, device_id=(0, chan), device_id_type=MESH)

    shard = tm * 8 + chan
    prior = jnp.maximum(shard - 1, 0)
    start_in = jnp.where(shard > 0, starts[prior], 0)
    width_in = jnp.where(shard > 0, widths[prior], 2)
    transfer[...] = transfer_matrix(
        emissions[...], labels, start_in, width_in, starts[shard], widths[shard], states
    )

    @pl.when(root)
    def _():
        pl.semaphore_wait(barrier, 7 + 7 + 15)

    @pl.when(jnp.logical_not(root))
    def _():
        pl.semaphore_wait(barrier, 7 + 8)

    copies = []
    for d in range(1, 8):
        copy = pltpu.make_async_remote_copy(
            src_ref=transfer, dst_ref=group.at[chan], send_sem=ts.at[d - 1], recv_sem=tr.at[d - 1],
            device_id=(tm, lax.rem(chan + d, 8)), device_id_type=MESH,
        )
        copy.start()
        copies.append(copy)
    group[chan] = transfer[...]
    for copy in copies:
        copy.wait_recv()

    span = group[0, pl.ds(pl.multiple_of(chan * 16, 16), 16), :]

    def grow(m, span):
        best = span[:, 0:1] + group[m, 0:1, :]
        for i in range(1, 128):
            best = jnp.maximum(best, span[:, i : i + 1] + group[m, i : i + 1, :])
        return best

    rows[...] = lax.fori_loop(1, 8, grow, span)
    for copy in copies:
        copy.wait_send()

    at = pl.ds(pl.multiple_of(tm * 128 + chan * 16, 16), 16)
    for c in range(8):

        @pl.when(jnp.logical_not(jnp.logical_and(root, chan == c)))
        def _():
            pltpu.make_async_remote_copy(
                src_ref=rows, dst_ref=spans.at[at], send_sem=ps.at[c], recv_sem=pr,
                device_id=(0, c), device_id_type=MESH,
            ).start()

    @pl.when(root)
    def _():
        spans[at, :] = rows[...]
        row = jnp.zeros((1, 128), jnp.float32)
        entry[...] = jnp.broadcast_to(row, (8, 128))
        others = spans.at[pl.ds(0, 127 * 16)]
        pltpu.make_async_copy(others, others, pr).wait()

        def chain(g, row):
            row = advance(row_to_column(row), spans[pl.ds(pl.multiple_of(g * 128, 128), 128), :])
            entries[g] = jnp.broadcast_to(row, (8, 128))
            pltpu.make_async_remote_copy(
                src_ref=entries.at[g], dst_ref=entry, send_sem=es.at[g], recv_sem=er,
                device_id=(g + 1, chan), device_id_type=MESH,
            ).start()
            return row

        lax.fori_loop(0, 15, chain, row)

    @pl.when(jnp.logical_not(root))
    def _():
        pltpu.make_async_copy(entry, entry, er).wait()

    row = lax.fori_loop(0, chan + 1, lambda m, row: advance(row_to_column(row), group[m]), entry[0:1, :])
    out[...] = jnp.where(row > 0.5 * NEG, row * (1.0 / 32768), 0.0)

    @pl.when(root)
    def _():
        def sent(g, carry):
            pltpu.make_async_copy(entries.at[g], entries.at[g], es.at[g]).wait()
            return carry

        lax.fori_loop(0, 15, sent, 0)

    for c in range(8):

        @pl.when(jnp.logical_not(jnp.logical_and(root, chan == c)))
        def _():
            pltpu.make_async_copy(rows, rows, ps.at[c]).wait()


def path_part(starts, widths, labels, emissions):
    dma = pltpu.SemaphoreType.DMA
    smem = pl.BlockSpec(memory_space=pltpu.SMEM)
    return pl.pallas_call(
        path_kernel,
        out_shape=jax.ShapeDtypeStruct((1, 128), jnp.float32),
        in_specs=[smem, smem, VM, VM],
        out_specs=VM,
        scratch_shapes=[
            pltpu.VMEM((264, 128), jnp.float32),
            pltpu.VMEM((128, 128), jnp.float32),
            pltpu.VMEM((8, 128, 128), jnp.float32),
            pltpu.VMEM((16, 128), jnp.float32),
            pltpu.VMEM((2048, 128), jnp.float32),
            pltpu.VMEM((8, 128), jnp.float32),
            pltpu.VMEM((16, 8, 128), jnp.float32),
            dma((7,)), dma((7,)), dma((8,)), dma, dma((16,)), dma,
        ],
        compiler_params=pltpu.CompilerParams(collective_id=2, has_side_effects=True, vmem_limit_bytes=24 * MIB),
        name="path",
    )(starts, widths, labels, emissions)


def local(frames, up_weight, down_weight, ffn_gain, final_gain, ctc_weight, labels, starts, widths):
    emissions = block_part(
        frames.T, up_weight, down_weight.T, ffn_gain.reshape(10, 128), final_gain.reshape(10, 128), ctc_weight
    )
    return emissions, path_part(starts, widths, labels.reshape(64, 128), emissions)


def solution(mesh):
    in_specs = (P("tm", "chan"), P("tm", "chan"), P("chan", "tm"), P(), P(), P(), P(), P(), P())
    out_specs = (P(("tm", "chan"), None), P(("tm", "chan"), None))
    return jax.shard_map(local, mesh=mesh, in_specs=in_specs, out_specs=out_specs, check_vma=False)
```

```python
import functools

import jax
import jax.numpy as jnp
from jax import lax
from jax.experimental import pallas as pl
from jax.experimental.pallas import tpu as pltpu
from jax.sharding import PartitionSpec as P

BAND = 128
LN_EPSILON = 1e-05
NEG = -1e30
MESH = pl.DeviceIdType.MESH
ANY = pl.BlockSpec(memory_space=pl.ANY)
HBM = pl.BlockSpec(memory_space=pltpu.HBM)
VM = pl.BlockSpec(memory_space=pltpu.VMEM)
MIB = 2**20


def position():
    tm, chan = lax.axis_index("tm"), lax.axis_index("chan")
    x = lax.rem(chan, 2) * 2 + tm // 8
    return x, lax.rem(tm // 2, 4), chan // 2, lax.rem(tm, 2)


def device(x, y, z, core):
    return (lax.rem(x, 2) * 8 + y * 2 + core, z * 2 + x // 2)


def moved(pos, axis, by):
    out = list(pos)
    out[axis] = lax.rem(pos[axis] + by + 4, 4)
    return tuple(out)


PARTS = (
    (0, 64, (2, 0, 1)), (64, 48, (1, 2, 0)), (112, 48, (0, 1, 2)),
)
ALL = (0, 1, 2)
ORDER = (
    (0, 0, 1), (0, 0, 2), (0, 0, 3), (0, 1, 1), (0, 1, 2), (0, 1, 3), (0, 2, 1), (0, 2, 2), (0, 2, 3), (1, 0, 0, 1),
    (1, 0, 0, 2), (1, 1, 0, 1), (1, 1, 0, 2), (1, 2, 0, 1), (1, 2, 0, 2), (7, 0, 1), (1, 0, 1, 1), (1, 0, 1, 2),
    (7, 1, 1), (1, 1, 1, 1), (1, 1, 1, 2), (7, 2, 1), (1, 2, 1, 1), (1, 2, 1, 2), (7, 0, 2), (1, 0, 2, 1),
    (1, 0, 2, 2), (7, 1, 2), (1, 1, 2, 1), (1, 1, 2, 2), (7, 2, 2), (1, 2, 2, 1), (1, 2, 2, 2), (7, 0, 3),
    (1, 0, 3, 1), (1, 0, 3, 2), (7, 1, 3), (1, 1, 3, 1), (1, 1, 3, 2), (7, 2, 3), (1, 2, 3, 1), (1, 2, 3, 2),
    (2, 0, 0, 1), (2, 0, 0, 2), (2, 1, 0, 1), (2, 1, 0, 2), (2, 2, 0, 1), (2, 2, 0, 2), (8, 0, 0, 1), (4, 0, 0, 1),
    (8, 0, 1, 1), (8, 0, 2, 1), (4, 0, 2, 1), (8, 0, 3, 1), (2, 0, 1, 1), (2, 0, 1, 2), (8, 1, 0, 1), (4, 1, 0, 1),
    (8, 1, 1, 1), (8, 1, 2, 1), (4, 1, 2, 1), (8, 1, 3, 1), (2, 1, 1, 1), (2, 1, 1, 2), (8, 2, 0, 1), (4, 2, 0, 1),
    (8, 2, 1, 1), (8, 2, 2, 1), (4, 2, 2, 1), (8, 2, 3, 1), (2, 2, 1, 1), (2, 2, 1, 2), (6,), (8, 0, 0, 2),
    (8, 0, 1, 2), (4, 0, 1, 2), (8, 0, 2, 2), (8, 0, 3, 2), (4, 0, 3, 2), (2, 0, 2, 1), (2, 0, 2, 2), (8, 1, 0, 2),
    (8, 1, 1, 2), (4, 1, 1, 2), (8, 1, 2, 2), (8, 1, 3, 2), (4, 1, 3, 2), (2, 1, 2, 1), (2, 1, 2, 2), (8, 2, 0, 2),
    (8, 2, 1, 2), (4, 2, 1, 2), (8, 2, 2, 2), (8, 2, 3, 2), (4, 2, 3, 2), (2, 2, 2, 1), (2, 2, 2, 2), (8, 0, 0, 3),
    (8, 0, 1, 3), (8, 0, 2, 3), (8, 0, 3, 3), (2, 0, 3, 1), (2, 0, 3, 2), (8, 1, 0, 3), (8, 1, 1, 3), (8, 1, 2, 3),
    (8, 1, 3, 3), (2, 1, 3, 1), (2, 1, 3, 2), (8, 2, 0, 3), (8, 2, 1, 3), (8, 2, 2, 3), (8, 2, 3, 3), (2, 2, 3, 1),
    (2, 2, 3, 2), (9, 0, 0, 1), (5, 0, 0, 1), (9, 1, 0, 1), (5, 1, 0, 1), (9, 2, 0, 1), (5, 2, 0, 1), (9, 0, 1, 1),
    (9, 1, 1, 1), (9, 2, 1, 1), (9, 0, 2, 1), (5, 0, 2, 1), (9, 1, 2, 1), (5, 1, 2, 1), (9, 2, 2, 1), (5, 2, 2, 1),
    (9, 0, 3, 1), (9, 1, 3, 1), (9, 2, 3, 1), (9, 0, 0, 2), (9, 1, 0, 2), (9, 2, 0, 2), (9, 0, 1, 2), (5, 0, 1, 2),
    (9, 1, 1, 2), (5, 1, 1, 2), (9, 2, 1, 2), (5, 2, 1, 2), (9, 0, 2, 2), (9, 1, 2, 2), (9, 2, 2, 2), (9, 0, 3, 2),
    (5, 0, 3, 2), (9, 1, 3, 2), (5, 1, 3, 2), (9, 2, 3, 2), (5, 2, 3, 2), (10,), (9, 0, 0, 3), (9, 0, 1, 3),
    (9, 0, 2, 3), (9, 2, 0, 3), (9, 2, 1, 3), (9, 2, 2, 3), (9, 2, 3, 3), (9, 0, 3, 3), (9, 1, 0, 3), (9, 1, 1, 3),
    (9, 1, 2, 3), (9, 1, 3, 3),
)
STEPS = (0, -1, 1, 2)
NT = (((1,), (1,)), ((), ()))


def block_at(w, pos, part):
    x, y, z, core = pos
    row, rows, _ = part
    return w.at[z, x // 2, lax.rem(x, 2), y, core, pl.ds(row, rows)]


def column_at(w, pos, part):
    x, y, z, core = pos
    row, rows, (axis, _, _) = part
    if axis == 0:
        return w.at[z, :, :, y, core, pl.ds(row, rows)]
    if axis == 1:
        return w.at[z, x // 2, lax.rem(x, 2), :, core, pl.ds(row, rows)]
    return w.at[:, x // 2, lax.rem(x, 2), y, core, pl.ds(row, rows)]


def slab_at(w, pos, part):
    x, y, z, core = pos
    row, rows, (_, _, axis) = part
    if axis == 0:
        return w.at[:, x // 2, lax.rem(x, 2), :, core, pl.ds(row, rows)]
    if axis == 1:
        return w.at[:, :, :, y, core, pl.ds(row, rows)]
    return w.at[z, :, :, :, core, pl.ds(row, rows)]


def norm_rows(values, gain_row):
    row_mean = jnp.mean(values, axis=-1, keepdims=True)
    centred = values - row_mean
    row_var = jnp.mean(jnp.square(centred), axis=-1, keepdims=True)
    return centred * lax.rsqrt(row_var + LN_EPSILON) * gain_row


def gain_row(ref):
    return jnp.concatenate([ref[k : k + 1, :] for k in range(10)], axis=1)


def block_kernel(
    frames, up, down, ffn_gain_hbm, final_gain_hbm, ctc_hbm, emis,
    w, mine, ctc, ffn_gain, final_gain, x_in, normed_in, total,
    local_sem, fr_send, fr_recv, s1, r1, s2, r2, s3, r3, sc, rc,
):
    me = position()
    x, y, z, core = me
    tm, chan = lax.axis_index("tm"), lax.axis_index("chan")
    sibling = (tm + 1 - 2 * core, chan)

    barrier = pltpu.get_barrier_semaphore()
    for axis in range(3):
        for by in (1, -1, 2):
            pl.semaphore_signal(barrier, inc=1, device_id=device(*moved(me, axis, by)), device_id_type=MESH)
    pl.semaphore_signal(barrier, inc=1, device_id=sibling, device_id_type=MESH)
    for d in range(1, 8):
        pl.semaphore_signal(barrier, inc=1, device_id=(tm, lax.rem(chan + d, 8)), device_id_type=MESH)
    here = w.at[z, x // 2, lax.rem(x, 2), y, core]
    locals_ = [
        pltpu.make_async_copy(up, here.at[pl.ds(0, 80)], local_sem.at[0]),
        pltpu.make_async_copy(down, here.at[pl.ds(80, 80)], local_sem.at[1]),
        pltpu.make_async_copy(frames.at[:, pl.ds(pl.multiple_of(chan * 256, 256), 256)], mine.at[chan], local_sem.at[2]),
        pltpu.make_async_copy(ctc_hbm, ctc, local_sem.at[3]),
        pltpu.make_async_copy(ffn_gain_hbm, ffn_gain, local_sem.at[4]),
        pltpu.make_async_copy(final_gain_hbm, final_gain, local_sem.at[5]),
    ]
    for copy in locals_:
        copy.start()
    locals_[0].wait()
    locals_[1].wait()
    pl.semaphore_wait(barrier, 17)

    pending = []

    def send(ref, send_sem, recv_sem, to, dst=None):
        copy = pltpu.make_async_remote_copy(
            src_ref=ref, dst_ref=ref if dst is None else dst, send_sem=send_sem, recv_sem=recv_sem,
            device_id=to, device_id_type=MESH,
        )
        copy.start()
        pending.append(copy)

    def arrived(ref, sem):
        pltpu.make_async_copy(ref, ref, sem).wait()

    def both_ways(ref, axis, send_sems, recv_sems):
        send(ref, send_sems(0), recv_sems(1), device(*moved(me, axis, 1)))
        send(ref, send_sems(1), recv_sems(2), device(*moved(me, axis, -1)))

    def to_sibling(p, k, ref):
        send(ref, sc.at[p, k], rc.at[p, k], sibling)

    def step_to(pos, axis, place):
        return moved(pos, axis, STEPS[place])

    def send_to(ref, axis, q, send_sem, recv_sem):
        send(ref, send_sem, recv_sem, device(*moved(me, axis, (1, -1, 2)[q - 1])))

    arrivals = {}

    def count(key, full):
        arrivals[key] = arrivals.get(key, 0) + 1
        return arrivals[key] == full

    def communicate(event):
        kind, p, *at = event
        part = PARTS[p]
        a, b, c = part[2]
        if kind == 0:
            (q,) = at
            send_to(block_at(w, me, part), a, q, s1.at[p, q - 1], r1.at[p, q])
        elif kind == 1:
            k, q = at
            send_to(block_at(w, step_to(me, a, k), part), b, q, s2.at[p, k, q - 1], r2.at[p, k, q])
        elif kind == 2:
            j, q = at
            send_to(column_at(w, step_to(me, b, j), part), c, q, s3.at[p, j, q - 1], r3.at[p, j, q])
        elif kind == 3:
            (k,) = at
            send_to(block_at(w, step_to(me, a, k), part), a, k, s1.at[p, 2], r1.at[p, 3])
        elif kind == 4:
            k, j = at
            send_to(block_at(w, step_to(step_to(me, b, j), a, k), part), b, j, s2.at[p, k, 2], r2.at[p, k, 3])
        elif kind == 5:
            j, i = at
            send_to(column_at(w, step_to(step_to(me, c, i), b, j), part), c, i, s3.at[p, j, 2], r3.at[p, j, 3])
        elif kind == 7:
            (k,) = at
            arrived(block_at(w, step_to(me, a, k), part), r1.at[p, k])
            if count((p, 0), 15):
                to_sibling(p, 0, slab_at(w, me, part))
        elif kind == 8:
            k, j = at
            arrived(block_at(w, step_to(step_to(me, b, j), a, k), part), r2.at[p, k, j])
            if count((p, 0), 15):
                to_sibling(p, 0, slab_at(w, me, part))
        elif kind == 9:
            j, i = at
            there = step_to(step_to(me, c, i), b, j)
            column = column_at(w, there, part)
            arrived(column, r3.at[p, j, i])
            if i == 3:
                to_sibling(p, 3 + j, column)
            elif count((p, i), 4):
                to_sibling(p, i, slab_at(w, there, part))

    other = (x, y, z, 1 - core)

    def slab_from_sibling(i, p):
        c = PARTS[p][2][2]
        arrived(slab_at(w, moved(other, c, STEPS[i]), PARTS[p]), rc.at[p, i])

    def from_sibling(j, p):
        _, b, c = PARTS[p][2]
        arrived(column_at(w, moved(moved(other, c, 2), b, STEPS[j]), PARTS[p]), rc.at[p, 3 + j])

    def send_frames():
        for d in range(1, 8):
            peer = lax.rem(chan + d, 8)
            send(
                frames.at[:, pl.ds(pl.multiple_of(peer * 256, 256), 256)], fr_send.at[d - 1], fr_recv.at[d - 1],
                (tm, peer), mine.at[chan],
            )

    def norm_frames():
        locals_[2].wait()
        locals_[4].wait()
        for d in range(1, 8):
            arrived(mine.at[lax.rem(chan + 8 - d, 8)], fr_recv.at[d - 1])
        x_in[...] = jnp.transpose(mine[...].astype(jnp.float32).reshape(1280, 256))
        normed_in[...] = norm_rows(x_in[...], gain_row(ffn_gain)).astype(jnp.bfloat16)
        total[...] = jnp.zeros_like(total)

    def project(first_step, count, xx):
        def one(q, carry):
            zz = lax.rem(z + q, 4)
            up_all = w[zz, xx, :, :, :, 0:80, :].reshape(1280, 640)
            down_all = w[zz, xx, :, :, :, 80:160, :].reshape(1280, 640)
            pre = jnp.dot(normed_in[...], up_all, preferred_element_type=jnp.float32)
            half = 0.5 * pre
            hidden = (half + half * jnp.tanh(half)).astype(jnp.bfloat16)
            total[...] += lax.dot_general(hidden, down_all, NT, preferred_element_type=jnp.float32)
            return carry

        lax.fori_loop(first_step, first_step + count, one, 0)

    for event in ORDER:
        if event[0] == 6:
            send_frames()
        elif event[0] == 10:
            norm_frames()
        else:
            communicate(event)
    on_y, on_x, on_z = ALL
    for p in ALL:
        for i in range(3):
            slab_from_sibling(i, p)
    for j in (0, 1, 2):
        from_sibling(j, on_y)
    project(3, 3, x // 2)
    for j in range(4):
        from_sibling(j, on_z)
    project(2, 1, x // 2)
    from_sibling(3, on_y)
    for j in range(4):
        from_sibling(j, on_x)
    project(0, 4, 1 - x // 2)

    locals_[3].wait()
    locals_[5].wait()
    residual = x_in[...] + 0.5 * total[...]
    normed = norm_rows(residual, gain_row(final_gain)).astype(jnp.bfloat16)
    logits = jnp.dot(normed, ctc[...], preferred_element_type=jnp.float32)
    shifted = logits - jnp.max(logits, axis=-1, keepdims=True)
    emis[...] = shifted - jnp.log(jnp.sum(jnp.exp(shifted), axis=-1, keepdims=True))
    for copy in pending:
        copy.wait_send()


def block_part(frames, up, down, ffn_gain, final_gain, ctc):
    dma = pltpu.SemaphoreType.DMA
    return pl.pallas_call(
        block_kernel,
        out_shape=jax.ShapeDtypeStruct((256, 256), jnp.float32),
        in_specs=[HBM] * 6,
        out_specs=VM,
        scratch_shapes=[
            pltpu.VMEM((4, 2, 2, 4, 2, 160, 640), jnp.bfloat16),
            pltpu.VMEM((8, 160, 256), jnp.bfloat16),
            pltpu.VMEM((1280, 256), jnp.bfloat16),
            pltpu.VMEM((10, 128), jnp.float32),
            pltpu.VMEM((10, 128), jnp.float32),
            pltpu.VMEM((256, 1280), jnp.float32),
            pltpu.VMEM((256, 1280), jnp.bfloat16),
            pltpu.VMEM((256, 1280), jnp.float32),
            dma((6,)), dma((7,)), dma((7,)),
            dma((3, 3)), dma((3, 4)),
            dma((3, 4, 3)), dma((3, 4, 4)),
            dma((3, 4, 3)), dma((3, 4, 4)),
            dma((3, 7)), dma((3, 7)),
        ],
        compiler_params=pltpu.CompilerParams(collective_id=1, has_side_effects=True, vmem_limit_bytes=62 * MIB),
        name="block",
    )(frames, up, down, ffn_gain, final_gain, ctc)


def split(values):
    high = values.astype(jnp.bfloat16)
    return high, (values - high.astype(jnp.float32)).astype(jnp.bfloat16)


def state_ids(labels, base):
    row0 = jnp.minimum(base // 128, 61)
    window = jnp.concatenate([labels[pl.ds(row0 + k, 1), :] for k in range(3)], axis=1)
    r = lax.broadcasted_iota(jnp.int32, (128, 384), 0)
    lane = lax.broadcasted_iota(jnp.int32, (128, 384), 1)
    at = base - row0 * 128 + 2 * ((r % 8) * 16 + r // 8) + 1
    pick = lambda here: jnp.sum(jnp.where(lane == here, window, 0), axis=1, keepdims=True)
    return pick(at), pick(at - 2)


def transfer_matrix(emissions, labels, start_in, width_in, start_out, width_out, states):
    par = lax.rem(start_in, 2)
    offset = start_out - start_in
    ids, ids_before = state_ids(labels, start_in - par)
    char = lax.broadcasted_iota(jnp.int32, (128, 256), 1)
    choose = ((ids == char).astype(jnp.float32) - (char == 0).astype(jnp.float32)).astype(jnp.bfloat16)
    high, low = split(emissions)
    rest = (emissions - high.astype(jnp.float32) - low.astype(jnp.float32)).astype(jnp.bfloat16)
    gain = sum(lax.dot_general(choose, part, NT, preferred_element_type=jnp.float32) for part in (high, low, rest))
    blank = jnp.sum(emissions[:, 0:1])
    skip = jnp.broadcast_to(jnp.where(ids == ids_before, NEG, 0.0), (128, 128)).reshape(16, 8, 128)
    v = lax.broadcasted_iota(jnp.int32, (16, 8, 128), 0)
    sub = lax.broadcasted_iota(jnp.int32, (16, 8, 128), 1)
    start = lax.broadcasted_iota(jnp.int32, (16, 8, 128), 2)
    at = 2 * (sub * 16 + v) - par
    live = start < width_in
    even = jnp.where((at == start) & live, 0.0, NEG)
    odd = jnp.where((at + 1 == start) & live, 0.0, NEG)
    top = jnp.full((8, 128), NEG, jnp.float32)
    first = lax.broadcasted_iota(jnp.int32, (8, 128), 0) == 0
    for half in range(2):
        block = gain[:, half * 128 : half * 128 + 128].reshape(16, 8, 128)
        for t in range(128):
            step = jnp.broadcast_to(block[:, :, t : t + 1], (16, 8, 128))
            turned = pltpu.roll(odd[15], 1, 0)
            below = jnp.concatenate([jnp.where(first, NEG, turned)[None], odd[:15]], axis=0)
            top = jnp.maximum(top, turned)
            odd = jnp.maximum(jnp.maximum(odd, even), below + skip) + step
            even = jnp.maximum(even, below)
    for k in range(16):
        states[pl.ds(2 * k, 8, stride=32), :] = even[k]
        states[pl.ds(2 * k + 1, 8, stride=32), :] = odd[k]
    states[256:264, :] = top
    reached = states[pl.ds(par + offset, 128), :]
    row = lax.broadcasted_iota(jnp.int32, (128, 128), 0)
    reached = jnp.where(row < width_out, reached + blank, NEG)
    return jnp.transpose(reached)


def row_to_column(row):
    i = lax.broadcasted_iota(jnp.int32, (128, 128), 0)
    j = lax.broadcasted_iota(jnp.int32, (128, 128), 1)
    return jnp.max(jnp.where(i == j, jnp.broadcast_to(row, (128, 128)), 4 * NEG), axis=1, keepdims=True)


def advance(column, matrix):
    return jnp.max(column + matrix, axis=0, keepdims=True)


def path_kernel(
    starts, widths, labels, emissions, out, states, transfer, group, rows, spans, entry, entries,
    ts, tr, ps, pr, es, er,
):
    tm, chan = lax.axis_index("tm"), lax.axis_index("chan")
    root = tm == 0
    barrier = pltpu.get_barrier_semaphore()
    for d in range(1, 8):
        pl.semaphore_signal(barrier, inc=1, device_id=(tm, lax.rem(chan + d, 8)), device_id_type=MESH)

    @pl.when(root)
    def _():
        def greet(g, carry):
            for d in range(8):

                @pl.when(jnp.logical_or(g != 0, d != 0))
                def _():
                    pl.semaphore_signal(barrier, inc=1, device_id=(g, lax.rem(chan + d, 8)), device_id_type=MESH)

            return carry

        lax.fori_loop(0, 16, greet, 0)

    @pl.when(jnp.logical_not(root))
    def _():
        pl.semaphore_signal(barrier, inc=1, device_id=(0, chan), device_id_type=MESH)

    shard = tm * 8 + chan
    prior = jnp.maximum(shard - 1, 0)
    start_in = jnp.where(shard > 0, starts[prior], 0)
    width_in = jnp.where(shard > 0, widths[prior], 2)
    transfer[...] = transfer_matrix(
        emissions[...], labels, start_in, width_in, starts[shard], widths[shard], states
    )

    @pl.when(root)
    def _():
        pl.semaphore_wait(barrier, 7 + 7 + 15)

    @pl.when(jnp.logical_not(root))
    def _():
        pl.semaphore_wait(barrier, 7 + 8)

    copies = []
    for d in range(1, 8):
        copy = pltpu.make_async_remote_copy(
            src_ref=transfer, dst_ref=group.at[chan], send_sem=ts.at[d - 1], recv_sem=tr.at[d - 1],
            device_id=(tm, lax.rem(chan + d, 8)), device_id_type=MESH,
        )
        copy.start()
        copies.append(copy)
    group[chan] = transfer[...]
    for copy in copies:
        copy.wait_recv()

    span = group[0, pl.ds(pl.multiple_of(chan * 16, 16), 16), :]

    def grow(m, span):
        best = span[:, 0:1] + group[m, 0:1, :]
        for i in range(1, 128):
            best = jnp.maximum(best, span[:, i : i + 1] + group[m, i : i + 1, :])
        return best

    rows[...] = lax.fori_loop(1, 8, grow, span)
    for copy in copies:
        copy.wait_send()

    at = pl.ds(pl.multiple_of(tm * 128 + chan * 16, 16), 16)
    for c in range(8):

        @pl.when(jnp.logical_not(jnp.logical_and(root, chan == c)))
        def _():
            pltpu.make_async_remote_copy(
                src_ref=rows, dst_ref=spans.at[at], send_sem=ps.at[c], recv_sem=pr,
                device_id=(0, c), device_id_type=MESH,
            ).start()

    @pl.when(root)
    def _():
        spans[at, :] = rows[...]
        row = jnp.zeros((1, 128), jnp.float32)
        entry[...] = jnp.broadcast_to(row, (8, 128))
        others = spans.at[pl.ds(0, 127 * 16)]
        pltpu.make_async_copy(others, others, pr).wait()

        def chain(g, row):
            row = advance(row_to_column(row), spans[pl.ds(pl.multiple_of(g * 128, 128), 128), :])
            entries[g] = jnp.broadcast_to(row, (8, 128))
            pltpu.make_async_remote_copy(
                src_ref=entries.at[g], dst_ref=entry, send_sem=es.at[g], recv_sem=er,
                device_id=(g + 1, chan), device_id_type=MESH,
            ).start()
            return row

        lax.fori_loop(0, 15, chain, row)

    @pl.when(jnp.logical_not(root))
    def _():
        pltpu.make_async_copy(entry, entry, er).wait()

    row = lax.fori_loop(0, chan + 1, lambda m, row: advance(row_to_column(row), group[m]), entry[0:1, :])
    out[...] = jnp.where(row > 0.5 * NEG, row * (1.0 / 32768), 0.0)

    @pl.when(root)
    def _():
        def sent(g, carry):
            pltpu.make_async_copy(entries.at[g], entries.at[g], es.at[g]).wait()
            return carry

        lax.fori_loop(0, 15, sent, 0)

    for c in range(8):

        @pl.when(jnp.logical_not(jnp.logical_and(root, chan == c)))
        def _():
            pltpu.make_async_copy(rows, rows, ps.at[c]).wait()


def path_part(starts, widths, labels, emissions):
    dma = pltpu.SemaphoreType.DMA
    smem = pl.BlockSpec(memory_space=pltpu.SMEM)
    return pl.pallas_call(
        path_kernel,
        out_shape=jax.ShapeDtypeStruct((1, 128), jnp.float32),
        in_specs=[smem, smem, VM, VM],
        out_specs=VM,
        scratch_shapes=[
            pltpu.VMEM((264, 128), jnp.float32),
            pltpu.VMEM((128, 128), jnp.float32),
            pltpu.VMEM((8, 128, 128), jnp.float32),
            pltpu.VMEM((16, 128), jnp.float32),
            pltpu.VMEM((2048, 128), jnp.float32),
            pltpu.VMEM((8, 128), jnp.float32),
            pltpu.VMEM((16, 8, 128), jnp.float32),
            dma((7,)), dma((7,)), dma((8,)), dma, dma((16,)), dma,
        ],
        compiler_params=pltpu.CompilerParams(collective_id=2, has_side_effects=True, vmem_limit_bytes=24 * MIB),
        name="path",
    )(starts, widths, labels, emissions)


def local(frames, up_weight, down_weight, ffn_gain, final_gain, ctc_weight, labels, starts, widths):
    emissions = block_part(
        frames.T, up_weight, down_weight.T, ffn_gain.reshape(10, 128), final_gain.reshape(10, 128), ctc_weight
    )
    return emissions, path_part(starts, widths, labels.reshape(64, 128), emissions)


def solution(mesh):
    in_specs = (P("tm", "chan"), P("tm", "chan"), P("chan", "tm"), P(), P(), P(), P(), P(), P())
    out_specs = (P(("tm", "chan"), None), P(("tm", "chan"), None))
    return jax.shard_map(local, mesh=mesh, in_specs=in_specs, out_specs=out_specs, check_vma=False)
```

```python
import functools

import jax
import jax.numpy as jnp
from jax import lax
from jax.experimental import pallas as pl
from jax.experimental.pallas import tpu as pltpu
from jax.sharding import PartitionSpec as P

BAND = 128
LN_EPSILON = 1e-05
NEG = -1e30
MESH = pl.DeviceIdType.MESH
ANY = pl.BlockSpec(memory_space=pl.ANY)
HBM = pl.BlockSpec(memory_space=pltpu.HBM)
VM = pl.BlockSpec(memory_space=pltpu.VMEM)
MIB = 2**20


def position():
    tm, chan = lax.axis_index("tm"), lax.axis_index("chan")
    x = lax.rem(chan, 2) * 2 + tm // 8
    return x, lax.rem(tm // 2, 4), chan // 2, lax.rem(tm, 2)


def device(x, y, z, core):
    return (lax.rem(x, 2) * 8 + y * 2 + core, z * 2 + x // 2)


def moved(pos, axis, by):
    out = list(pos)
    out[axis] = lax.rem(pos[axis] + by + 4, 4)
    return tuple(out)


PARTS = (
    (0, 64, (2, 0, 1)), (64, 48, (1, 2, 0)), (112, 48, (0, 1, 2)),
)
ALL = (0, 1, 2)
ORDER = (
    (0, 0, 1), (0, 0, 2), (0, 0, 3), (0, 1, 1), (0, 1, 2), (0, 1, 3), (0, 2, 1), (0, 2, 2), (0, 2, 3), (1, 0, 0, 1),
    (1, 0, 0, 2), (1, 1, 0, 1), (1, 1, 0, 2), (1, 2, 0, 1), (1, 2, 0, 2), (7, 0, 1), (1, 0, 1, 1), (1, 0, 1, 2),
    (7, 1, 1), (1, 1, 1, 1), (1, 1, 1, 2), (7, 2, 1), (1, 2, 1, 1), (1, 2, 1, 2), (7, 0, 2), (1, 0, 2, 1),
    (1, 0, 2, 2), (7, 1, 2), (1, 1, 2, 1), (1, 1, 2, 2), (7, 2, 2), (1, 2, 2, 1), (1, 2, 2, 2), (7, 0, 3),
    (1, 0, 3, 1), (1, 0, 3, 2), (7, 1, 3), (1, 1, 3, 1), (1, 1, 3, 2), (7, 2, 3), (1, 2, 3, 1), (1, 2, 3, 2),
    (2, 0, 0, 1), (2, 0, 0, 2), (2, 1, 0, 1), (2, 1, 0, 2), (2, 2, 0, 1), (2, 2, 0, 2), (8, 0, 0, 1), (4, 0, 0, 1),
    (8, 0, 1, 1), (8, 0, 2, 1), (4, 0, 2, 1), (8, 0, 3, 1), (2, 0, 1, 1), (2, 0, 1, 2), (8, 1, 0, 1), (4, 1, 0, 1),
    (8, 1, 1, 1), (8, 1, 2, 1), (4, 1, 2, 1), (8, 1, 3, 1), (2, 1, 1, 1), (2, 1, 1, 2), (8, 2, 0, 1), (4, 2, 0, 1),
    (8, 2, 1, 1), (8, 2, 2, 1), (4, 2, 2, 1), (8, 2, 3, 1), (2, 2, 1, 1), (2, 2, 1, 2), (6,), (8, 0, 0, 2),
    (8, 0, 1, 2), (4, 0, 1, 2), (8, 0, 2, 2), (8, 0, 3, 2), (4, 0, 3, 2), (2, 0, 2, 1), (2, 0, 2, 2), (8, 1, 0, 2),
    (8, 1, 1, 2), (4, 1, 1, 2), (8, 1, 2, 2), (8, 1, 3, 2), (4, 1, 3, 2), (2, 1, 2, 1), (2, 1, 2, 2), (8, 2, 0, 2),
    (8, 2, 1, 2), (4, 2, 1, 2), (8, 2, 2, 2), (8, 2, 3, 2), (4, 2, 3, 2), (2, 2, 2, 1), (2, 2, 2, 2), (8, 0, 0, 3),
    (8, 0, 1, 3), (8, 0, 2, 3), (8, 0, 3, 3), (2, 0, 3, 1), (2, 0, 3, 2), (8, 1, 0, 3), (8, 1, 1, 3), (8, 1, 2, 3),
    (8, 1, 3, 3), (2, 1, 3, 1), (2, 1, 3, 2), (8, 2, 0, 3), (8, 2, 1, 3), (8, 2, 2, 3), (8, 2, 3, 3), (2, 2, 3, 1),
    (2, 2, 3, 2), (9, 0, 0, 1), (5, 0, 0, 1), (9, 0, 0, 2), (9, 1, 0, 1), (5, 1, 0, 1), (9, 1, 0, 2), (9, 2, 0, 1),
    (5, 2, 0, 1), (9, 2, 0, 2), (9, 0, 1, 1), (9, 0, 1, 2), (5, 0, 1, 2), (9, 1, 1, 1), (9, 1, 1, 2), (5, 1, 1, 2),
    (9, 2, 1, 1), (9, 2, 1, 2), (5, 2, 1, 2), (9, 0, 2, 1), (5, 0, 2, 1), (9, 0, 2, 2), (9, 1, 2, 1), (5, 1, 2, 1),
    (9, 1, 2, 2), (9, 2, 2, 1), (5, 2, 2, 1), (9, 2, 2, 2), (9, 0, 3, 1), (9, 0, 3, 2), (5, 0, 3, 2), (9, 1, 3, 1),
    (9, 1, 3, 2), (5, 1, 3, 2), (9, 2, 3, 1), (9, 2, 3, 2), (5, 2, 3, 2), (10,), (9, 0, 0, 3), (9, 0, 1, 3),
    (9, 0, 2, 3), (9, 2, 0, 3), (9, 2, 1, 3), (9, 2, 2, 3), (9, 2, 3, 3), (9, 0, 3, 3), (9, 1, 0, 3), (9, 1, 1, 3),
    (9, 1, 2, 3), (9, 1, 3, 3),
)
STEPS = (0, -1, 1, 2)
NT = (((1,), (1,)), ((), ()))


def block_at(w, pos, part):
    x, y, z, core = pos
    row, rows, _ = part
    return w.at[z, x // 2, lax.rem(x, 2), y, core, pl.ds(row, rows)]


def column_at(w, pos, part):
    x, y, z, core = pos
    row, rows, (axis, _, _) = part
    if axis == 0:
        return w.at[z, :, :, y, core, pl.ds(row, rows)]
    if axis == 1:
        return w.at[z, x // 2, lax.rem(x, 2), :, core, pl.ds(row, rows)]
    return w.at[:, x // 2, lax.rem(x, 2), y, core, pl.ds(row, rows)]


def slab_at(w, pos, part):
    x, y, z, core = pos
    row, rows, (_, _, axis) = part
    if axis == 0:
        return w.at[:, x // 2, lax.rem(x, 2), :, core, pl.ds(row, rows)]
    if axis == 1:
        return w.at[:, :, :, y, core, pl.ds(row, rows)]
    return w.at[z, :, :, :, core, pl.ds(row, rows)]


def norm_rows(values, gain_row):
    row_mean = jnp.mean(values, axis=-1, keepdims=True)
    centred = values - row_mean
    row_var = jnp.mean(jnp.square(centred), axis=-1, keepdims=True)
    return centred * lax.rsqrt(row_var + LN_EPSILON) * gain_row


def gain_row(ref):
    return jnp.concatenate([ref[k : k + 1, :] for k in range(10)], axis=1)


def block_kernel(
    frames, up, down, ffn_gain_hbm, final_gain_hbm, ctc_hbm, emis,
    w, mine, ctc, ffn_gain, final_gain, x_in, normed_in, total,
    local_sem, fr_send, fr_recv, s1, r1, s2, r2, s3, r3, sc, rc,
):
    me = position()
    x, y, z, core = me
    tm, chan = lax.axis_index("tm"), lax.axis_index("chan")
    sibling = (tm + 1 - 2 * core, chan)

    barrier = pltpu.get_barrier_semaphore()
    for axis in range(3):
        for by in (1, -1, 2):
            pl.semaphore_signal(barrier, inc=1, device_id=device(*moved(me, axis, by)), device_id_type=MESH)
    pl.semaphore_signal(barrier, inc=1, device_id=sibling, device_id_type=MESH)
    for d in range(1, 8):
        pl.semaphore_signal(barrier, inc=1, device_id=(tm, lax.rem(chan + d, 8)), device_id_type=MESH)
    here = w.at[z, x // 2, lax.rem(x, 2), y, core]
    locals_ = [
        pltpu.make_async_copy(up, here.at[pl.ds(0, 80)], local_sem.at[0]),
        pltpu.make_async_copy(down, here.at[pl.ds(80, 80)], local_sem.at[1]),
        pltpu.make_async_copy(frames.at[:, pl.ds(pl.multiple_of(chan * 256, 256), 256)], mine.at[chan], local_sem.at[2]),
        pltpu.make_async_copy(ctc_hbm, ctc, local_sem.at[3]),
        pltpu.make_async_copy(ffn_gain_hbm, ffn_gain, local_sem.at[4]),
        pltpu.make_async_copy(final_gain_hbm, final_gain, local_sem.at[5]),
    ]
    for copy in locals_:
        copy.start()
    locals_[0].wait()
    locals_[1].wait()
    pl.semaphore_wait(barrier, 17)

    pending = []

    def send(ref, send_sem, recv_sem, to, dst=None):
        copy = pltpu.make_async_remote_copy(
            src_ref=ref, dst_ref=ref if dst is None else dst, send_sem=send_sem, recv_sem=recv_sem,
            device_id=to, device_id_type=MESH,
        )
        copy.start()
        pending.append(copy)

    def arrived(ref, sem):
        pltpu.make_async_copy(ref, ref, sem).wait()

    def both_ways(ref, axis, send_sems, recv_sems):
        send(ref, send_sems(0), recv_sems(1), device(*moved(me, axis, 1)))
        send(ref, send_sems(1), recv_sems(2), device(*moved(me, axis, -1)))

    def to_sibling(p, k, ref):
        send(ref, sc.at[p, k], rc.at[p, k], sibling)

    def step_to(pos, axis, place):
        return moved(pos, axis, STEPS[place])

    def send_to(ref, axis, q, send_sem, recv_sem):
        send(ref, send_sem, recv_sem, device(*moved(me, axis, (1, -1, 2)[q - 1])))

    arrivals = {}

    def count(key, full):
        arrivals[key] = arrivals.get(key, 0) + 1
        return arrivals[key] == full

    def communicate(event):
        kind, p, *at = event
        part = PARTS[p]
        a, b, c = part[2]
        if kind == 0:
            (q,) = at
            send_to(block_at(w, me, part), a, q, s1.at[p, q - 1], r1.at[p, q])
        elif kind == 1:
            k, q = at
            send_to(block_at(w, step_to(me, a, k), part), b, q, s2.at[p, k, q - 1], r2.at[p, k, q])
        elif kind == 2:
            j, q = at
            send_to(column_at(w, step_to(me, b, j), part), c, q, s3.at[p, j, q - 1], r3.at[p, j, q])
        elif kind == 3:
            (k,) = at
            send_to(block_at(w, step_to(me, a, k), part), a, k, s1.at[p, 2], r1.at[p, 3])
        elif kind == 4:
            k, j = at
            send_to(block_at(w, step_to(step_to(me, b, j), a, k), part), b, j, s2.at[p, k, 2], r2.at[p, k, 3])
        elif kind == 5:
            j, i = at
            send_to(column_at(w, step_to(step_to(me, c, i), b, j), part), c, i, s3.at[p, j, 2], r3.at[p, j, 3])
        elif kind == 7:
            (k,) = at
            arrived(block_at(w, step_to(me, a, k), part), r1.at[p, k])
            if count((p, 0), 15):
                to_sibling(p, 0, slab_at(w, me, part))
        elif kind == 8:
            k, j = at
            arrived(block_at(w, step_to(step_to(me, b, j), a, k), part), r2.at[p, k, j])
            if count((p, 0), 15):
                to_sibling(p, 0, slab_at(w, me, part))
        elif kind == 9:
            j, i = at
            there = step_to(step_to(me, c, i), b, j)
            column = column_at(w, there, part)
            arrived(column, r3.at[p, j, i])
            if i == 3:
                to_sibling(p, 3 + j, column)
            elif count((p, i), 4):
                to_sibling(p, i, slab_at(w, there, part))

    other = (x, y, z, 1 - core)

    def slab_from_sibling(i, p):
        c = PARTS[p][2][2]
        arrived(slab_at(w, moved(other, c, STEPS[i]), PARTS[p]), rc.at[p, i])

    def from_sibling(j, p):
        _, b, c = PARTS[p][2]
        arrived(column_at(w, moved(moved(other, c, 2), b, STEPS[j]), PARTS[p]), rc.at[p, 3 + j])

    def send_frames():
        for d in range(1, 8):
            peer = lax.rem(chan + d, 8)
            send(
                frames.at[:, pl.ds(pl.multiple_of(peer * 256, 256), 256)], fr_send.at[d - 1], fr_recv.at[d - 1],
                (tm, peer), mine.at[chan],
            )

    def norm_frames():
        locals_[2].wait()
        locals_[4].wait()
        for d in range(1, 8):
            arrived(mine.at[lax.rem(chan + 8 - d, 8)], fr_recv.at[d - 1])
        x_in[...] = jnp.transpose(mine[...].astype(jnp.float32).reshape(1280, 256))
        normed_in[...] = norm_rows(x_in[...], gain_row(ffn_gain)).astype(jnp.bfloat16)
        total[...] = jnp.zeros_like(total)

    def project(first_step, count, xx):
        def one(q, carry):
            zz = lax.rem(z + q, 4)
            up_all = w[zz, xx, :, :, :, 0:80, :].reshape(1280, 640)
            down_all = w[zz, xx, :, :, :, 80:160, :].reshape(1280, 640)
            pre = jnp.dot(normed_in[...], up_all, preferred_element_type=jnp.float32)
            half = 0.5 * pre
            hidden = (half + half * jnp.tanh(half)).astype(jnp.bfloat16)
            total[...] += lax.dot_general(hidden, down_all, NT, preferred_element_type=jnp.float32)
            return carry

        lax.fori_loop(first_step, first_step + count, one, 0)

    for event in ORDER:
        if event[0] == 6:
            send_frames()
        elif event[0] == 10:
            norm_frames()
        else:
            communicate(event)
    on_y, on_x, on_z = ALL
    for p in ALL:
        for i in range(3):
            slab_from_sibling(i, p)
    for j in (0, 1, 2):
        from_sibling(j, on_y)
    project(3, 3, x // 2)
    for j in range(4):
        from_sibling(j, on_z)
    project(2, 1, x // 2)
    from_sibling(3, on_y)
    for j in range(4):
        from_sibling(j, on_x)
    project(0, 4, 1 - x // 2)

    locals_[3].wait()
    locals_[5].wait()
    residual = x_in[...] + 0.5 * total[...]
    normed = norm_rows(residual, gain_row(final_gain)).astype(jnp.bfloat16)
    logits = jnp.dot(normed, ctc[...], preferred_element_type=jnp.float32)
    shifted = logits - jnp.max(logits, axis=-1, keepdims=True)
    emis[...] = shifted - jnp.log(jnp.sum(jnp.exp(shifted), axis=-1, keepdims=True))
    for copy in pending:
        copy.wait_send()


def block_part(frames, up, down, ffn_gain, final_gain, ctc):
    dma = pltpu.SemaphoreType.DMA
    return pl.pallas_call(
        block_kernel,
        out_shape=jax.ShapeDtypeStruct((256, 256), jnp.float32),
        in_specs=[HBM] * 6,
        out_specs=VM,
        scratch_shapes=[
            pltpu.VMEM((4, 2, 2, 4, 2, 160, 640), jnp.bfloat16),
            pltpu.VMEM((8, 160, 256), jnp.bfloat16),
            pltpu.VMEM((1280, 256), jnp.bfloat16),
            pltpu.VMEM((10, 128), jnp.float32),
            pltpu.VMEM((10, 128), jnp.float32),
            pltpu.VMEM((256, 1280), jnp.float32),
            pltpu.VMEM((256, 1280), jnp.bfloat16),
            pltpu.VMEM((256, 1280), jnp.float32),
            dma((6,)), dma((7,)), dma((7,)),
            dma((3, 3)), dma((3, 4)),
            dma((3, 4, 3)), dma((3, 4, 4)),
            dma((3, 4, 3)), dma((3, 4, 4)),
            dma((3, 7)), dma((3, 7)),
        ],
        compiler_params=pltpu.CompilerParams(collective_id=1, has_side_effects=True, vmem_limit_bytes=62 * MIB),
        name="block",
    )(frames, up, down, ffn_gain, final_gain, ctc)


def split(values):
    high = values.astype(jnp.bfloat16)
    return high, (values - high.astype(jnp.float32)).astype(jnp.bfloat16)


def state_ids(labels, base):
    row0 = jnp.minimum(base // 128, 61)
    window = jnp.concatenate([labels[pl.ds(row0 + k, 1), :] for k in range(3)], axis=1)
    r = lax.broadcasted_iota(jnp.int32, (128, 384), 0)
    lane = lax.broadcasted_iota(jnp.int32, (128, 384), 1)
    at = base - row0 * 128 + 2 * ((r % 8) * 16 + r // 8) + 1
    pick = lambda here: jnp.sum(jnp.where(lane == here, window, 0), axis=1, keepdims=True)
    return pick(at), pick(at - 2)


def transfer_matrix(emissions, labels, start_in, width_in, start_out, width_out, states):
    par = lax.rem(start_in, 2)
    offset = start_out - start_in
    ids, ids_before = state_ids(labels, start_in - par)
    char = lax.broadcasted_iota(jnp.int32, (128, 256), 1)
    choose = ((ids == char).astype(jnp.float32) - (char == 0).astype(jnp.float32)).astype(jnp.bfloat16)
    high, low = split(emissions)
    rest = (emissions - high.astype(jnp.float32) - low.astype(jnp.float32)).astype(jnp.bfloat16)
    gain = sum(lax.dot_general(choose, part, NT, preferred_element_type=jnp.float32) for part in (high, low, rest))
    blank = jnp.sum(emissions[:, 0:1])
    skip = jnp.broadcast_to(jnp.where(ids == ids_before, NEG, 0.0), (128, 128)).reshape(16, 8, 128)
    v = lax.broadcasted_iota(jnp.int32, (16, 8, 128), 0)
    sub = lax.broadcasted_iota(jnp.int32, (16, 8, 128), 1)
    start = lax.broadcasted_iota(jnp.int32, (16, 8, 128), 2)
    at = 2 * (sub * 16 + v) - par
    live = start < width_in
    even = jnp.where((at == start) & live, 0.0, NEG)
    odd = jnp.where((at + 1 == start) & live, 0.0, NEG)
    top = jnp.full((8, 128), NEG, jnp.float32)
    first = lax.broadcasted_iota(jnp.int32, (8, 128), 0) == 0
    for half in range(2):
        block = gain[:, half * 128 : half * 128 + 128].reshape(16, 8, 128)
        for t in range(128):
            step = jnp.broadcast_to(block[:, :, t : t + 1], (16, 8, 128))
            turned = pltpu.roll(odd[15], 1, 0)
            below = jnp.concatenate([jnp.where(first, NEG, turned)[None], odd[:15]], axis=0)
            top = jnp.maximum(top, turned)
            odd = jnp.maximum(jnp.maximum(odd, even), below + skip) + step
            even = jnp.maximum(even, below)
    for k in range(16):
        states[pl.ds(2 * k, 8, stride=32), :] = even[k]
        states[pl.ds(2 * k + 1, 8, stride=32), :] = odd[k]
    states[256:264, :] = top
    reached = states[pl.ds(par + offset, 128), :]
    row = lax.broadcasted_iota(jnp.int32, (128, 128), 0)
    reached = jnp.where(row < width_out, reached + blank, NEG)
    return jnp.transpose(reached)


def row_to_column(row):
    i = lax.broadcasted_iota(jnp.int32, (128, 128), 0)
    j = lax.broadcasted_iota(jnp.int32, (128, 128), 1)
    return jnp.max(jnp.where(i == j, jnp.broadcast_to(row, (128, 128)), 4 * NEG), axis=1, keepdims=True)


def advance(column, matrix):
    return jnp.max(column + matrix, axis=0, keepdims=True)


def path_kernel(
    starts, widths, labels, emissions, out, states, transfer, group, rows, spans, entry, entries,
    ts, tr, ps, pr, es, er,
):
    tm, chan = lax.axis_index("tm"), lax.axis_index("chan")
    root = tm == 0
    barrier = pltpu.get_barrier_semaphore()
    for d in range(1, 8):
        pl.semaphore_signal(barrier, inc=1, device_id=(tm, lax.rem(chan + d, 8)), device_id_type=MESH)

    @pl.when(root)
    def _():
        members = [lax.rem(chan + d, 8) for d in range(8)]

        def greet(g, carry):
            for member in members:
                pl.semaphore_signal(barrier, inc=1, device_id=(g, member), device_id_type=MESH)
            return carry

        lax.fori_loop(1, 16, greet, 0)

    @pl.when(jnp.logical_not(root))
    def _():
        pl.semaphore_signal(barrier, inc=1, device_id=(0, chan), device_id_type=MESH)

    shard = tm * 8 + chan
    prior = jnp.maximum(shard - 1, 0)
    start_in = jnp.where(shard > 0, starts[prior], 0)
    width_in = jnp.where(shard > 0, widths[prior], 2)
    transfer[...] = transfer_matrix(
        emissions[...], labels, start_in, width_in, starts[shard], widths[shard], states
    )

    @pl.when(root)
    def _():
        pl.semaphore_wait(barrier, 7 + 15)

    @pl.when(jnp.logical_not(root))
    def _():
        pl.semaphore_wait(barrier, 7 + 8)

    copies = []
    for d in range(1, 8):
        copy = pltpu.make_async_remote_copy(
            src_ref=transfer, dst_ref=group.at[chan], send_sem=ts.at[d - 1], recv_sem=tr.at[chan],
            device_id=(tm, lax.rem(chan + d, 8)), device_id_type=MESH,
        )
        copy.start()
        copies.append(copy)
    group[chan] = transfer[...]

    def await_member(m):
        @pl.when(m != chan)
        def _():
            pltpu.make_async_copy(group.at[m], group.at[m], tr.at[m]).wait()

    await_member(0)
    span = group[0, pl.ds(pl.multiple_of(chan * 16, 16), 16), :]

    def grow(m, span):
        await_member(m)
        best = span[:, 0:1] + group[m, 0:1, :]
        for i in range(1, 128):
            best = jnp.maximum(best, span[:, i : i + 1] + group[m, i : i + 1, :])
        return best

    rows[...] = lax.fori_loop(1, 8, grow, span)
    for copy in copies:
        copy.wait_send()

    at = pl.ds(pl.multiple_of(tm * 128 + chan * 16, 16), 16)
    for c in range(8):

        @pl.when(jnp.logical_not(jnp.logical_and(root, chan == c)))
        def _():
            pltpu.make_async_remote_copy(
                src_ref=rows, dst_ref=spans.at[at], send_sem=ps.at[c], recv_sem=pr,
                device_id=(0, c), device_id_type=MESH,
            ).start()

    @pl.when(root)
    def _():
        spans[at, :] = rows[...]
        row = jnp.zeros((1, 128), jnp.float32)
        entry[...] = jnp.broadcast_to(row, (8, 128))
        others = spans.at[pl.ds(0, 127 * 16)]
        pltpu.make_async_copy(others, others, pr).wait()

        def chain(g, row):
            row = advance(row_to_column(row), spans[pl.ds(pl.multiple_of(g * 128, 128), 128), :])
            entries[g] = jnp.broadcast_to(row, (8, 128))
            pltpu.make_async_remote_copy(
                src_ref=entries.at[g], dst_ref=entry, send_sem=es.at[g], recv_sem=er,
                device_id=(g + 1, chan), device_id_type=MESH,
            ).start()
            return row

        lax.fori_loop(0, 15, chain, row)

    @pl.when(jnp.logical_not(root))
    def _():
        pltpu.make_async_copy(entry, entry, er).wait()

    row = lax.fori_loop(0, chan + 1, lambda m, row: advance(row_to_column(row), group[m]), entry[0:1, :])
    out[...] = jnp.where(row > 0.5 * NEG, row * (1.0 / 32768), 0.0)

    @pl.when(root)
    def _():
        def sent(g, carry):
            pltpu.make_async_copy(entries.at[g], entries.at[g], es.at[g]).wait()
            return carry

        lax.fori_loop(0, 15, sent, 0)

    for c in range(8):

        @pl.when(jnp.logical_not(jnp.logical_and(root, chan == c)))
        def _():
            pltpu.make_async_copy(rows, rows, ps.at[c]).wait()


def path_part(starts, widths, labels, emissions):
    dma = pltpu.SemaphoreType.DMA
    smem = pl.BlockSpec(memory_space=pltpu.SMEM)
    return pl.pallas_call(
        path_kernel,
        out_shape=jax.ShapeDtypeStruct((1, 128), jnp.float32),
        in_specs=[smem, smem, VM, VM],
        out_specs=VM,
        scratch_shapes=[
            pltpu.VMEM((264, 128), jnp.float32),
            pltpu.VMEM((128, 128), jnp.float32),
            pltpu.VMEM((8, 128, 128), jnp.float32),
            pltpu.VMEM((16, 128), jnp.float32),
            pltpu.VMEM((2048, 128), jnp.float32),
            pltpu.VMEM((8, 128), jnp.float32),
            pltpu.VMEM((16, 8, 128), jnp.float32),
            dma((7,)), dma((8,)), dma((8,)), dma, dma((16,)), dma,
        ],
        compiler_params=pltpu.CompilerParams(collective_id=2, has_side_effects=True, vmem_limit_bytes=24 * MIB),
        name="path",
    )(starts, widths, labels, emissions)


def local(frames, up_weight, down_weight, ffn_gain, final_gain, ctc_weight, labels, starts, widths):
    emissions = block_part(
        frames.T, up_weight, down_weight.T, ffn_gain.reshape(10, 128), final_gain.reshape(10, 128), ctc_weight
    )
    return emissions, path_part(starts, widths, labels.reshape(64, 128), emissions)


def solution(mesh):
    in_specs = (P("tm", "chan"), P("tm", "chan"), P("chan", "tm"), P(), P(), P(), P(), P(), P())
    out_specs = (P(("tm", "chan"), None), P(("tm", "chan"), None))
    return jax.shard_map(local, mesh=mesh, in_specs=in_specs, out_specs=out_specs, check_vma=False)
```

```python
import functools

import jax
import jax.numpy as jnp
from jax import lax
from jax.experimental import pallas as pl
from jax.experimental.pallas import tpu as pltpu
from jax.sharding import PartitionSpec as P

BAND = 128
LN_EPSILON = 1e-05
NEG = -1e30
MESH = pl.DeviceIdType.MESH
ANY = pl.BlockSpec(memory_space=pl.ANY)
HBM = pl.BlockSpec(memory_space=pltpu.HBM)
VM = pl.BlockSpec(memory_space=pltpu.VMEM)
MIB = 2**20


def position():
    tm, chan = lax.axis_index("tm"), lax.axis_index("chan")
    x = lax.rem(chan, 2) * 2 + tm // 8
    return x, lax.rem(tm // 2, 4), chan // 2, lax.rem(tm, 2)


def device(x, y, z, core):
    return (lax.rem(x, 2) * 8 + y * 2 + core, z * 2 + x // 2)


def moved(pos, axis, by):
    out = list(pos)
    out[axis] = lax.rem(pos[axis] + by + 4, 4)
    return tuple(out)


PARTS = (
    (0, 64, (2, 0, 1)), (64, 48, (1, 2, 0)), (112, 48, (0, 1, 2)),
)
ALL = (0, 1, 2)
ORDER = (
    (0, 0, 3), (0, 1, 3), (0, 2, 3), (0, 0, 1), (0, 0, 2), (0, 1, 1), (0, 1, 2), (0, 2, 1), (0, 2, 2), (1, 0, 0, 1),
    (1, 0, 0, 2), (1, 1, 0, 1), (1, 1, 0, 2), (1, 2, 0, 1), (1, 2, 0, 2), (7, 0, 1), (1, 0, 1, 1), (1, 0, 1, 2),
    (7, 1, 1), (1, 1, 1, 1), (1, 1, 1, 2), (7, 2, 1), (1, 2, 1, 1), (1, 2, 1, 2), (7, 0, 2), (1, 0, 2, 1),
    (1, 0, 2, 2), (7, 1, 2), (1, 1, 2, 1), (1, 1, 2, 2), (7, 2, 2), (1, 2, 2, 1), (1, 2, 2, 2), (7, 0, 3),
    (1, 0, 3, 1), (1, 0, 3, 2), (7, 1, 3), (1, 1, 3, 1), (1, 1, 3, 2), (7, 2, 3), (1, 2, 3, 1), (1, 2, 3, 2),
    (2, 0, 0, 1), (2, 0, 0, 2), (2, 1, 0, 1), (2, 1, 0, 2), (2, 2, 0, 1), (2, 2, 0, 2), (8, 0, 0, 1), (4, 0, 0, 1),
    (8, 0, 1, 1), (8, 0, 2, 1), (4, 0, 2, 1), (8, 0, 3, 1), (2, 0, 1, 1), (2, 0, 1, 2), (8, 1, 0, 1), (4, 1, 0, 1),
    (8, 1, 1, 1), (8, 1, 2, 1), (4, 1, 2, 1), (8, 1, 3, 1), (2, 1, 1, 1), (2, 1, 1, 2), (8, 2, 0, 1), (4, 2, 0, 1),
    (8, 2, 1, 1), (8, 2, 2, 1), (4, 2, 2, 1), (8, 2, 3, 1), (2, 2, 1, 1), (2, 2, 1, 2), (6,), (8, 0, 0, 2),
    (8, 0, 1, 2), (4, 0, 1, 2), (8, 0, 2, 2), (8, 0, 3, 2), (4, 0, 3, 2), (2, 0, 2, 1), (2, 0, 2, 2), (8, 1, 0, 2),
    (8, 1, 1, 2), (4, 1, 1, 2), (8, 1, 2, 2), (8, 1, 3, 2), (4, 1, 3, 2), (2, 1, 2, 1), (2, 1, 2, 2), (8, 2, 0, 2),
    (8, 2, 1, 2), (4, 2, 1, 2), (8, 2, 2, 2), (8, 2, 3, 2), (4, 2, 3, 2), (2, 2, 2, 1), (2, 2, 2, 2), (8, 0, 0, 3),
    (8, 0, 1, 3), (8, 0, 2, 3), (8, 0, 3, 3), (2, 0, 3, 1), (2, 0, 3, 2), (8, 1, 0, 3), (8, 1, 1, 3), (8, 1, 2, 3),
    (8, 1, 3, 3), (2, 1, 3, 1), (2, 1, 3, 2), (8, 2, 0, 3), (8, 2, 1, 3), (8, 2, 2, 3), (8, 2, 3, 3), (2, 2, 3, 1),
    (2, 2, 3, 2), (9, 0, 0, 1), (5, 0, 0, 1), (9, 0, 0, 2), (9, 1, 0, 1), (5, 1, 0, 1), (9, 1, 0, 2), (9, 2, 0, 1),
    (5, 2, 0, 1), (9, 2, 0, 2), (9, 0, 1, 1), (9, 0, 1, 2), (5, 0, 1, 2), (9, 1, 1, 1), (9, 1, 1, 2), (5, 1, 1, 2),
    (9, 2, 1, 1), (9, 2, 1, 2), (5, 2, 1, 2), (9, 0, 2, 1), (5, 0, 2, 1), (9, 0, 2, 2), (9, 1, 2, 1), (5, 1, 2, 1),
    (9, 1, 2, 2), (9, 2, 2, 1), (5, 2, 2, 1), (9, 2, 2, 2), (9, 0, 3, 1), (9, 0, 3, 2), (5, 0, 3, 2), (9, 1, 3, 1),
    (9, 1, 3, 2), (5, 1, 3, 2), (9, 2, 3, 1), (9, 2, 3, 2), (5, 2, 3, 2), (10,), (9, 0, 0, 3), (9, 0, 1, 3),
    (9, 0, 2, 3), (9, 2, 0, 3), (9, 2, 1, 3), (9, 2, 2, 3), (9, 2, 3, 3), (9, 0, 3, 3), (9, 1, 0, 3), (9, 1, 1, 3),
    (9, 1, 2, 3), (9, 1, 3, 3),
)
STEPS = (0, -1, 1, 2)
NT = (((1,), (1,)), ((), ()))


def block_at(w, pos, part):
    x, y, z, core = pos
    row, rows, _ = part
    return w.at[z, x // 2, lax.rem(x, 2), y, core, pl.ds(row, rows)]


def column_at(w, pos, part):
    x, y, z, core = pos
    row, rows, (axis, _, _) = part
    if axis == 0:
        return w.at[z, :, :, y, core, pl.ds(row, rows)]
    if axis == 1:
        return w.at[z, x // 2, lax.rem(x, 2), :, core, pl.ds(row, rows)]
    return w.at[:, x // 2, lax.rem(x, 2), y, core, pl.ds(row, rows)]


def slab_at(w, pos, part):
    x, y, z, core = pos
    row, rows, (_, _, axis) = part
    if axis == 0:
        return w.at[:, x // 2, lax.rem(x, 2), :, core, pl.ds(row, rows)]
    if axis == 1:
        return w.at[:, :, :, y, core, pl.ds(row, rows)]
    return w.at[z, :, :, :, core, pl.ds(row, rows)]


def norm_rows(values, gain_row):
    row_mean = jnp.mean(values, axis=-1, keepdims=True)
    centred = values - row_mean
    row_var = jnp.mean(jnp.square(centred), axis=-1, keepdims=True)
    return centred * lax.rsqrt(row_var + LN_EPSILON) * gain_row


def gain_row(ref):
    return jnp.concatenate([ref[k : k + 1, :] for k in range(10)], axis=1)


def block_kernel(
    frames, up, down, ffn_gain_hbm, final_gain_hbm, ctc_hbm, emis,
    w, mine, ctc, ffn_gain, final_gain, x_in, normed_in, total,
    local_sem, fr_send, fr_recv, s1, r1, s2, r2, s3, r3, sc, rc,
):
    me = position()
    x, y, z, core = me
    tm, chan = lax.axis_index("tm"), lax.axis_index("chan")
    sibling = (tm + 1 - 2 * core, chan)

    barrier = pltpu.get_barrier_semaphore()
    for axis in range(3):
        for by in (1, -1, 2):
            pl.semaphore_signal(barrier, inc=1, device_id=device(*moved(me, axis, by)), device_id_type=MESH)
    pl.semaphore_signal(barrier, inc=1, device_id=sibling, device_id_type=MESH)
    for d in range(1, 8):
        pl.semaphore_signal(barrier, inc=1, device_id=(tm, lax.rem(chan + d, 8)), device_id_type=MESH)
    here = w.at[z, x // 2, lax.rem(x, 2), y, core]
    locals_ = [
        pltpu.make_async_copy(up, here.at[pl.ds(0, 80)], local_sem.at[0]),
        pltpu.make_async_copy(down, here.at[pl.ds(80, 80)], local_sem.at[1]),
        pltpu.make_async_copy(frames.at[:, pl.ds(pl.multiple_of(chan * 256, 256), 256)], mine.at[chan], local_sem.at[2]),
        pltpu.make_async_copy(ctc_hbm, ctc, local_sem.at[3]),
        pltpu.make_async_copy(ffn_gain_hbm, ffn_gain, local_sem.at[4]),
        pltpu.make_async_copy(final_gain_hbm, final_gain, local_sem.at[5]),
    ]
    for copy in locals_:
        copy.start()
    locals_[0].wait()
    locals_[1].wait()
    pl.semaphore_wait(barrier, 17)

    pending = []

    def send(ref, send_sem, recv_sem, to, dst=None):
        copy = pltpu.make_async_remote_copy(
            src_ref=ref, dst_ref=ref if dst is None else dst, send_sem=send_sem, recv_sem=recv_sem,
            device_id=to, device_id_type=MESH,
        )
        copy.start()
        pending.append(copy)

    def arrived(ref, sem):
        pltpu.make_async_copy(ref, ref, sem).wait()

    def both_ways(ref, axis, send_sems, recv_sems):
        send(ref, send_sems(0), recv_sems(1), device(*moved(me, axis, 1)))
        send(ref, send_sems(1), recv_sems(2), device(*moved(me, axis, -1)))

    def to_sibling(p, k, ref):
        send(ref, sc.at[p, k], rc.at[p, k], sibling)

    def step_to(pos, axis, place):
        return moved(pos, axis, STEPS[place])

    def send_to(ref, axis, q, send_sem, recv_sem):
        send(ref, send_sem, recv_sem, device(*moved(me, axis, (1, -1, 2)[q - 1])))

    arrivals = {}

    def count(key, full):
        arrivals[key] = arrivals.get(key, 0) + 1
        return arrivals[key] == full

    def communicate(event):
        kind, p, *at = event
        part = PARTS[p]
        a, b, c = part[2]
        if kind == 0:
            (q,) = at
            send_to(block_at(w, me, part), a, q, s1.at[p, q - 1], r1.at[p, q])
        elif kind == 1:
            k, q = at
            send_to(block_at(w, step_to(me, a, k), part), b, q, s2.at[p, k, q - 1], r2.at[p, k, q])
        elif kind == 2:
            j, q = at
            send_to(column_at(w, step_to(me, b, j), part), c, q, s3.at[p, j, q - 1], r3.at[p, j, q])
        elif kind == 3:
            (k,) = at
            send_to(block_at(w, step_to(me, a, k), part), a, k, s1.at[p, 2], r1.at[p, 3])
        elif kind == 4:
            k, j = at
            send_to(block_at(w, step_to(step_to(me, b, j), a, k), part), b, j, s2.at[p, k, 2], r2.at[p, k, 3])
        elif kind == 5:
            j, i = at
            send_to(column_at(w, step_to(step_to(me, c, i), b, j), part), c, i, s3.at[p, j, 2], r3.at[p, j, 3])
        elif kind == 7:
            (k,) = at
            arrived(block_at(w, step_to(me, a, k), part), r1.at[p, k])
            if count((p, 0), 15):
                to_sibling(p, 0, slab_at(w, me, part))
        elif kind == 8:
            k, j = at
            arrived(block_at(w, step_to(step_to(me, b, j), a, k), part), r2.at[p, k, j])
            if count((p, 0), 15):
                to_sibling(p, 0, slab_at(w, me, part))
        elif kind == 9:
            j, i = at
            there = step_to(step_to(me, c, i), b, j)
            column = column_at(w, there, part)
            arrived(column, r3.at[p, j, i])
            if i == 3:
                to_sibling(p, 3 + j, column)
            elif count((p, i), 4):
                to_sibling(p, i, slab_at(w, there, part))

    other = (x, y, z, 1 - core)

    def slab_from_sibling(i, p):
        c = PARTS[p][2][2]
        arrived(slab_at(w, moved(other, c, STEPS[i]), PARTS[p]), rc.at[p, i])

    def from_sibling(j, p):
        _, b, c = PARTS[p][2]
        arrived(column_at(w, moved(moved(other, c, 2), b, STEPS[j]), PARTS[p]), rc.at[p, 3 + j])

    def send_frames():
        for d in range(1, 8):
            peer = lax.rem(chan + d, 8)
            send(
                frames.at[:, pl.ds(pl.multiple_of(peer * 256, 256), 256)], fr_send.at[d - 1], fr_recv.at[d - 1],
                (tm, peer), mine.at[chan],
            )

    def norm_frames():
        locals_[2].wait()
        locals_[4].wait()
        for d in range(1, 8):
            arrived(mine.at[lax.rem(chan + 8 - d, 8)], fr_recv.at[d - 1])
        x_in[...] = jnp.transpose(mine[...].astype(jnp.float32).reshape(1280, 256))
        normed_in[...] = norm_rows(x_in[...], gain_row(ffn_gain)).astype(jnp.bfloat16)
        total[...] = jnp.zeros_like(total)

    def project(first_step, count, xx):
        def one(q, carry):
            zz = lax.rem(z + q, 4)
            up_all = w[zz, xx, :, :, :, 0:80, :].reshape(1280, 640)
            down_all = w[zz, xx, :, :, :, 80:160, :].reshape(1280, 640)
            pre = jnp.dot(normed_in[...], up_all, preferred_element_type=jnp.float32)
            half = 0.5 * pre
            hidden = (half + half * jnp.tanh(half)).astype(jnp.bfloat16)
            total[...] += lax.dot_general(hidden, down_all, NT, preferred_element_type=jnp.float32)
            return carry

        lax.fori_loop(first_step, first_step + count, one, 0)

    for event in ORDER:
        if event[0] == 6:
            send_frames()
        elif event[0] == 10:
            norm_frames()
        else:
            communicate(event)
    on_y, on_x, on_z = ALL
    for p in ALL:
        for i in range(3):
            slab_from_sibling(i, p)
    for j in (0, 1, 2):
        from_sibling(j, on_y)
    project(3, 3, x // 2)
    for j in range(4):
        from_sibling(j, on_z)
    project(2, 1, x // 2)
    from_sibling(3, on_y)
    for j in range(4):
        from_sibling(j, on_x)
    project(0, 4, 1 - x // 2)

    locals_[3].wait()
    locals_[5].wait()
    residual = x_in[...] + 0.5 * total[...]
    normed = norm_rows(residual, gain_row(final_gain)).astype(jnp.bfloat16)
    logits = jnp.dot(normed, ctc[...], preferred_element_type=jnp.float32)
    shifted = logits - jnp.max(logits, axis=-1, keepdims=True)
    emis[...] = shifted - jnp.log(jnp.sum(jnp.exp(shifted), axis=-1, keepdims=True))
    for copy in pending:
        copy.wait_send()


def block_part(frames, up, down, ffn_gain, final_gain, ctc):
    dma = pltpu.SemaphoreType.DMA
    return pl.pallas_call(
        block_kernel,
        out_shape=jax.ShapeDtypeStruct((256, 256), jnp.float32),
        in_specs=[HBM] * 6,
        out_specs=VM,
        scratch_shapes=[
            pltpu.VMEM((4, 2, 2, 4, 2, 160, 640), jnp.bfloat16),
            pltpu.VMEM((8, 160, 256), jnp.bfloat16),
            pltpu.VMEM((1280, 256), jnp.bfloat16),
            pltpu.VMEM((10, 128), jnp.float32),
            pltpu.VMEM((10, 128), jnp.float32),
            pltpu.VMEM((256, 1280), jnp.float32),
            pltpu.VMEM((256, 1280), jnp.bfloat16),
            pltpu.VMEM((256, 1280), jnp.float32),
            dma((6,)), dma((7,)), dma((7,)),
            dma((3, 3)), dma((3, 4)),
            dma((3, 4, 3)), dma((3, 4, 4)),
            dma((3, 4, 3)), dma((3, 4, 4)),
            dma((3, 7)), dma((3, 7)),
        ],
        compiler_params=pltpu.CompilerParams(collective_id=1, has_side_effects=True, vmem_limit_bytes=62 * MIB),
        name="block",
    )(frames, up, down, ffn_gain, final_gain, ctc)


def split(values):
    high = values.astype(jnp.bfloat16)
    return high, (values - high.astype(jnp.float32)).astype(jnp.bfloat16)


def state_ids(labels, base):
    row0 = jnp.minimum(base // 128, 61)
    window = jnp.concatenate([labels[pl.ds(row0 + k, 1), :] for k in range(3)], axis=1)
    r = lax.broadcasted_iota(jnp.int32, (128, 384), 0)
    lane = lax.broadcasted_iota(jnp.int32, (128, 384), 1)
    at = base - row0 * 128 + 2 * ((r % 8) * 16 + r // 8) + 1
    pick = lambda here: jnp.sum(jnp.where(lane == here, window, 0), axis=1, keepdims=True)
    return pick(at), pick(at - 2)


def transfer_matrix(emissions, labels, start_in, width_in, start_out, width_out, states):
    par = lax.rem(start_in, 2)
    offset = start_out - start_in
    ids, ids_before = state_ids(labels, start_in - par)
    char = lax.broadcasted_iota(jnp.int32, (128, 256), 1)
    choose = ((ids == char).astype(jnp.float32) - (char == 0).astype(jnp.float32)).astype(jnp.bfloat16)
    high, low = split(emissions)
    rest = (emissions - high.astype(jnp.float32) - low.astype(jnp.float32)).astype(jnp.bfloat16)
    gain = sum(lax.dot_general(choose, part, NT, preferred_element_type=jnp.float32) for part in (high, low, rest))
    blank = jnp.sum(emissions[:, 0:1])
    skip = jnp.broadcast_to(jnp.where(ids == ids_before, NEG, 0.0), (128, 128)).reshape(16, 8, 128)
    v = lax.broadcasted_iota(jnp.int32, (16, 8, 128), 0)
    sub = lax.broadcasted_iota(jnp.int32, (16, 8, 128), 1)
    start = lax.broadcasted_iota(jnp.int32, (16, 8, 128), 2)
    at = 2 * (sub * 16 + v) - par
    live = start < width_in
    even = jnp.where((at == start) & live, 0.0, NEG)
    odd = jnp.where((at + 1 == start) & live, 0.0, NEG)
    top = jnp.full((8, 128), NEG, jnp.float32)
    first = lax.broadcasted_iota(jnp.int32, (8, 128), 0) == 0
    for half in range(2):
        block = gain[:, half * 128 : half * 128 + 128].reshape(16, 8, 128)
        for t in range(128):
            step = jnp.broadcast_to(block[:, :, t : t + 1], (16, 8, 128))
            turned = pltpu.roll(odd[15], 1, 0)
            below = jnp.concatenate([jnp.where(first, NEG, turned)[None], odd[:15]], axis=0)
            top = jnp.maximum(top, turned)
            odd = jnp.maximum(jnp.maximum(odd, even), below + skip) + step
            even = jnp.maximum(even, below)
    for k in range(16):
        states[pl.ds(2 * k, 8, stride=32), :] = even[k]
        states[pl.ds(2 * k + 1, 8, stride=32), :] = odd[k]
    states[256:264, :] = top
    reached = states[pl.ds(par + offset, 128), :]
    row = lax.broadcasted_iota(jnp.int32, (128, 128), 0)
    reached = jnp.where(row < width_out, reached + blank, NEG)
    return jnp.transpose(reached)


def row_to_column(row):
    i = lax.broadcasted_iota(jnp.int32, (128, 128), 0)
    j = lax.broadcasted_iota(jnp.int32, (128, 128), 1)
    return jnp.max(jnp.where(i == j, jnp.broadcast_to(row, (128, 128)), 4 * NEG), axis=1, keepdims=True)


def advance(column, matrix):
    return jnp.max(column + matrix, axis=0, keepdims=True)


def path_kernel(
    starts, widths, labels, emissions, out, states, transfer, group, rows, spans, entry, entries,
    ts, tr, ps, pr, es, er,
):
    tm, chan = lax.axis_index("tm"), lax.axis_index("chan")
    root = tm == 0
    barrier = pltpu.get_barrier_semaphore()
    for d in range(1, 8):
        pl.semaphore_signal(barrier, inc=1, device_id=(tm, lax.rem(chan + d, 8)), device_id_type=MESH)

    @pl.when(root)
    def _():
        members = [lax.rem(chan + d, 8) for d in range(8)]

        def greet(g, carry):
            for member in members:
                pl.semaphore_signal(barrier, inc=1, device_id=(g, member), device_id_type=MESH)
            return carry

        lax.fori_loop(1, 16, greet, 0)

    @pl.when(jnp.logical_not(root))
    def _():
        pl.semaphore_signal(barrier, inc=1, device_id=(0, chan), device_id_type=MESH)

    shard = tm * 8 + chan
    prior = jnp.maximum(shard - 1, 0)
    start_in = jnp.where(shard > 0, starts[prior], 0)
    width_in = jnp.where(shard > 0, widths[prior], 2)
    transfer[...] = transfer_matrix(
        emissions[...], labels, start_in, width_in, starts[shard], widths[shard], states
    )

    @pl.when(root)
    def _():
        pl.semaphore_wait(barrier, 7 + 15)

    @pl.when(jnp.logical_not(root))
    def _():
        pl.semaphore_wait(barrier, 7 + 8)

    copies = []
    for d in range(1, 8):
        copy = pltpu.make_async_remote_copy(
            src_ref=transfer, dst_ref=group.at[chan], send_sem=ts.at[d - 1], recv_sem=tr.at[chan],
            device_id=(tm, lax.rem(chan + d, 8)), device_id_type=MESH,
        )
        copy.start()
        copies.append(copy)
    group[chan] = transfer[...]

    def await_member(m):
        @pl.when(m != chan)
        def _():
            pltpu.make_async_copy(group.at[m], group.at[m], tr.at[m]).wait()

    await_member(0)
    span = group[0, pl.ds(pl.multiple_of(chan * 16, 16), 16), :]

    def grow(m, span):
        await_member(m)
        best = span[:, 0:1] + group[m, 0:1, :]
        for i in range(1, 128):
            best = jnp.maximum(best, span[:, i : i + 1] + group[m, i : i + 1, :])
        return best

    rows[...] = lax.fori_loop(1, 8, grow, span)
    for copy in copies:
        copy.wait_send()

    at = pl.ds(pl.multiple_of(tm * 128 + chan * 16, 16), 16)
    for c in range(8):

        @pl.when(jnp.logical_not(jnp.logical_and(root, chan == c)))
        def _():
            pltpu.make_async_remote_copy(
                src_ref=rows, dst_ref=spans.at[at], send_sem=ps.at[c], recv_sem=pr,
                device_id=(0, c), device_id_type=MESH,
            ).start()

    @pl.when(root)
    def _():
        spans[at, :] = rows[...]
        row = jnp.zeros((1, 128), jnp.float32)
        entry[...] = jnp.broadcast_to(row, (8, 128))
        others = spans.at[pl.ds(0, 127 * 16)]
        pltpu.make_async_copy(others, others, pr).wait()

        def chain(g, row):
            row = advance(row_to_column(row), spans[pl.ds(pl.multiple_of(g * 128, 128), 128), :])
            entries[g] = jnp.broadcast_to(row, (8, 128))
            pltpu.make_async_remote_copy(
                src_ref=entries.at[g], dst_ref=entry, send_sem=es.at[g], recv_sem=er,
                device_id=(g + 1, chan), device_id_type=MESH,
            ).start()
            return row

        lax.fori_loop(0, 15, chain, row)

    @pl.when(jnp.logical_not(root))
    def _():
        pltpu.make_async_copy(entry, entry, er).wait()

    row = lax.fori_loop(0, chan + 1, lambda m, row: advance(row_to_column(row), group[m]), entry[0:1, :])
    out[...] = jnp.where(row > 0.5 * NEG, row * (1.0 / 32768), 0.0)

    @pl.when(root)
    def _():
        def sent(g, carry):
            pltpu.make_async_copy(entries.at[g], entries.at[g], es.at[g]).wait()
            return carry

        lax.fori_loop(0, 15, sent, 0)

    for c in range(8):

        @pl.when(jnp.logical_not(jnp.logical_and(root, chan == c)))
        def _():
            pltpu.make_async_copy(rows, rows, ps.at[c]).wait()


def path_part(starts, widths, labels, emissions):
    dma = pltpu.SemaphoreType.DMA
    smem = pl.BlockSpec(memory_space=pltpu.SMEM)
    return pl.pallas_call(
        path_kernel,
        out_shape=jax.ShapeDtypeStruct((1, 128), jnp.float32),
        in_specs=[smem, smem, VM, VM],
        out_specs=VM,
        scratch_shapes=[
            pltpu.VMEM((264, 128), jnp.float32),
            pltpu.VMEM((128, 128), jnp.float32),
            pltpu.VMEM((8, 128, 128), jnp.float32),
            pltpu.VMEM((16, 128), jnp.float32),
            pltpu.VMEM((2048, 128), jnp.float32),
            pltpu.VMEM((8, 128), jnp.float32),
            pltpu.VMEM((16, 8, 128), jnp.float32),
            dma((7,)), dma((8,)), dma((8,)), dma, dma((16,)), dma,
        ],
        compiler_params=pltpu.CompilerParams(collective_id=2, has_side_effects=True, vmem_limit_bytes=24 * MIB),
        name="path",
    )(starts, widths, labels, emissions)


def local(frames, up_weight, down_weight, ffn_gain, final_gain, ctc_weight, labels, starts, widths):
    emissions = block_part(
        frames.T, up_weight, down_weight.T, ffn_gain.reshape(10, 128), final_gain.reshape(10, 128), ctc_weight
    )
    return emissions, path_part(starts, widths, labels.reshape(64, 128), emissions)


def solution(mesh):
    in_specs = (P("tm", "chan"), P("tm", "chan"), P("chan", "tm"), P(), P(), P(), P(), P(), P())
    out_specs = (P(("tm", "chan"), None), P(("tm", "chan"), None))
    return jax.shard_map(local, mesh=mesh, in_specs=in_specs, out_specs=out_specs, check_vma=False)
```
